32 devices in a mesh: member: 4 (over y, x), space: 8 (over z, core).
Axes of the slice: x: 2, y: 2, z: 4, core: 2. Of those that a mesh axis runs over, the one named last changes fastest.
Arguments:
- initial_fields: bfloat16 [128, 64, 1024], P('member', None, 'space'), may hold values from -4 to 4
- encode_weight: bfloat16 [64, 256], replicated, may hold values from -0.75 to 0.75
- send_weight: bfloat16 [1, 256, 256], replicated, may hold values from -0.375 to 0.375
- receive_weight: bfloat16 [1, 256, 256], replicated, may hold values from -0.375 to 0.375
- update_weight: bfloat16 [1, 256, 256], replicated, may hold values from -0.375 to 0.375
- norm_gain: bfloat16 [1, 256], replicated, may hold values from 0.099609375 to 1.8984375
- decode_weight: bfloat16 [256, 64], replicated, may hold values from -0.375 to 0.375
- edge_senders: int32 [1024, 4], P('space'), may hold values from 0 to 191
- halo_nodes: int32 [2, 256], P(None, 'space'), may hold values from 0 to 127, as said below
- observed_perturbation: bfloat16 [32, 128, 256], P(('member', 'space')), may hold values from -2.5 to 2.5
- observed_values: bfloat16 [32, 2, 256], P(('member', 'space')), may hold values from -3.5 to 3.5, as said below
- region_neighbours: int32 [32, 8], P(('member', 'space')), may hold values from 0 to 31, as said below
Outputs:
- analysis: bfloat16 [128, 64, 1024], P('member', None, 'space')
The draws below stay inside these ranges and needn't reach their ends.
Inputs may be any that keep to these rules, and one draw needn't show every extreme that they name: edge_senders[n, k] indexes the list of the 128 nodes of n's space block, followed by the 32 nodes that halo_nodes row 0 names in the block before and the 32 that row 1 names in the block after (blocks wrap around). For each space block b, halo_nodes[0, b * 32 : (b + 1) * 32] are distinct node indices within block b - 1 and halo_nodes[1, ...] distinct ones within block b + 1, taken modulo 8. `region_neighbours`: each row lists 8 distinct regions other than r = a * 8 + b; each is ((a + p) mod 4) * 8 + ((b + s) mod 8) with either p = 0 and 1 <= |s| <= 2, or |p| = 1 and |s| <= 1. `observed_values`: row 0 of each region holds positive inverse error variances of at least 0.25.
All inputs are finite; a program needn't handle non-finite values.
Results may differ from the reference program's by a relative error of at most 0.0059.
Values may be sent and summed in bfloat16 or wider, within the bound.
No kernel may reach another device: no remote copies, remote signals or barrier semaphores. Data moves between devices by JAX's collectives and lax.ppermute only.
A program may use at most 64 MiB of HBM per device.

```python
import math
import jax
import jax.numpy as jnp
import numpy as np
from jax import lax

H = 256
VERTEX_FEATURES = 64
NODE_DEV = 128
OBS_REG = 256
LAYERS = 1
ITERS_NS = 5
DEG = 4
NEIGH = 8
MEMBER_TOTAL = 128
NODES = 1024
HALO = 32
AREA_VERTICES = 32
AREA_LATITUDES = 4
AREA_LONGITUDES = 8
AREA_TOTAL = 32


ROW_SHIFTS = np.array([0, 0, 0, 0, -1, -1, -1, 1, 1, 1], np.int32)


COLUMN_SHIFTS = np.array([-2, -1, 1, 2, -1, 0, 1, -1, 0, 1], np.int32)


def draw_initial_fields(key, part):
    first = jax.random.fold_in(key, 0)
    noise = jax.random.normal(first, (MEMBER_TOTAL, VERTEX_FEATURES, NODES), jnp.float32)
    return jnp.clip(noise, -4.0, 4.0).astype(jnp.bfloat16)


def draw_observed_values(key, part):
    first, second = jax.random.split(key)
    lowest = math.log(0.25)
    highest = math.log(3.5)
    inverse_var = jnp.exp(jax.random.uniform(first, (AREA_TOTAL, 1, OBS_REG), jnp.float32, lowest, highest))
    innovation = jax.random.normal(second, (AREA_TOTAL, 1, OBS_REG), jnp.float32)
    innovation = jnp.clip(innovation, -3.5, 3.5)
    return jnp.concatenate([inverse_var, innovation], axis=1).astype(jnp.bfloat16)


def draw_halo_nodes(key, part):
    scores = jax.random.randint(key, (2, AREA_LONGITUDES, NODE_DEV), 0, 65536) * NODE_DEV + jnp.arange(NODE_DEV, dtype=jnp.int32)
    chosen = jnp.argsort(scores, axis=2)
    return chosen[:, :, :HALO].reshape(2, AREA_LONGITUDES * HALO).astype(jnp.int32)


def draw_region_neighbours(key, part):
    scores = jax.random.randint(key, (AREA_TOTAL, 10), 0, 65536) * 16 + jnp.arange(10, dtype=jnp.int32)
    chosen = jnp.argsort(scores, axis=1)[:, :NEIGH]
    region = jnp.arange(AREA_TOTAL, dtype=jnp.int32)[:, None]
    row_index = (region // AREA_LONGITUDES + jnp.asarray(ROW_SHIFTS)[chosen]) % AREA_LATITUDES
    column_index = (region % AREA_LONGITUDES + jnp.asarray(COLUMN_SHIFTS)[chosen]) % AREA_LONGITUDES
    return (row_index * AREA_LONGITUDES + column_index).astype(jnp.int32)


def place_ends(values, rng, least, largest):
    index_at = [jax.random.randint(jax.random.fold_in(rng, axis), (), 0, length) for axis, length in enumerate(values.shape)]
    widest = values.shape.index(max(values.shape))
    next_to = index_at[:widest] + [(index_at[widest] + 1) % values.shape[widest]] + index_at[widest + 1:]
    return values.at[tuple(index_at)].set(least).at[tuple(next_to)].set(largest)


def steps_of(rng, dims, cuts, least, top_value):
    def one(dim, shards_of):
        draws = jax.random.uniform(jax.random.fold_in(jax.random.fold_in(rng, 6), dim), (shards_of,), jnp.float32, least / len(cuts), top_value / len(cuts))
        return jnp.repeat(jnp.exp(draws), dims[dim] // shards_of).reshape((-1,) + (1,) * (len(dims) - dim - 1))

    gain = one(*cuts[0])
    for cut in cuts[1:]:
        gain = gain * one(*cut)
    return gain


def scatter_about(key, shape, width, most, pieces=(), kind=jnp.bfloat16):
    level = steps_of(key, shape, pieces, -0.22, 0.18) if pieces else 1.0
    drawn = jax.random.normal(key, shape, jnp.float32) * width * level
    return jnp.minimum(jnp.maximum(drawn, -most), most).astype(kind)


def setup_inputs(seed: int = 0) -> dict:
    streams_of = jax.random.split(jax.random.key(seed), 13)
    initial_fields = draw_initial_fields(jax.random.fold_in(streams_of[12], 71), 0)
    encode_weight = scatter_about(streams_of[1], (VERTEX_FEATURES, H), VERTEX_FEATURES ** -0.5, 0.75)
    send_weight = scatter_about(streams_of[2], (LAYERS, H, H), H ** -0.5, 0.375)
    receive_weight = scatter_about(streams_of[3], (LAYERS, H, H), H ** -0.5, 0.375)
    update_weight = scatter_about(streams_of[4], (LAYERS, H, H), H ** -0.5, 0.375)
    norm_gain = jnp.clip(1.0 + 0.18 * jax.random.normal(streams_of[5], (LAYERS, H), jnp.float32), 0.099609375, 1.8984375).astype(jnp.bfloat16)
    decode_weight = scatter_about(streams_of[6], (H, VERTEX_FEATURES), H ** -0.5, 0.375)
    edge_senders = place_ends(jax.random.randint(streams_of[7], (NODES, DEG), 0, NODE_DEV + 2 * HALO), jax.random.fold_in(streams_of[7], 1), 0, (NODE_DEV + 2 * HALO) - 1).astype(jnp.int32)
    halo_nodes = draw_halo_nodes(jax.random.fold_in(streams_of[12], 71), 0)
    observed_perturbation = scatter_about(streams_of[9], (AREA_TOTAL, MEMBER_TOTAL, OBS_REG), 0.3, 2.5, ((0, 32),))
    observed_values = draw_observed_values(jax.random.fold_in(streams_of[12], 71), 0)
    region_neighbours = draw_region_neighbours(jax.random.fold_in(streams_of[12], 71), 0)
    return {"initial_fields": initial_fields, "encode_weight": encode_weight, "send_weight": send_weight, "receive_weight": receive_weight, "update_weight": update_weight, "norm_gain": norm_gain, "decode_weight": decode_weight, "edge_senders": edge_senders, "halo_nodes": halo_nodes, "observed_perturbation": observed_perturbation, "observed_values": observed_values, "region_neighbours": region_neighbours}


EPSILON = 1e-05
FULL_PRECISION = lax.Precision.HIGHEST

def wide_dot(left, right):
    return jnp.dot(left.astype(jnp.float32), right.astype(jnp.float32), precision=FULL_PRECISION)

def normalize(messages, gains):
    mean_square = lax.optimization_barrier(jnp.mean(messages * messages, axis=-1, keepdims=True))
    return messages * lax.rsqrt(mean_square + EPSILON) * gains.astype(jnp.float32)

def inverse_root(system):
    extent = system.shape[0]
    identity = jnp.eye(extent, dtype=jnp.float32)
    scaling = jnp.sqrt(jnp.sum(system * system))
    iterate = system / scaling
    inverse = identity
    for _ in range(ITERS_NS):
        correction = 1.5 * identity - 0.5 * jnp.dot(inverse, iterate, precision=FULL_PRECISION)
        iterate = jnp.dot(iterate, correction, precision=FULL_PRECISION)
        inverse = jnp.dot(correction, inverse, precision=FULL_PRECISION)
    return (inverse, scaling)

def analyse(states, gram_matrix, forcing):
    ensemble = states.shape[0]
    identity = jnp.eye(ensemble, dtype=jnp.float32)
    system = identity + gram_matrix / (ensemble - 1)
    inverse, scaling = inverse_root(system)
    inner = jnp.dot(inverse, forcing, precision=FULL_PRECISION)
    mean_weights = jnp.dot(inverse, inner, precision=FULL_PRECISION) / (scaling * (ensemble - 1))
    transform = inverse / jnp.sqrt(scaling) + mean_weights[:, None]
    mean_state = lax.optimization_barrier(jnp.mean(states, axis=0))
    anomalies = states - mean_state
    moved = jnp.einsum('ij,is->js', transform, anomalies, precision=FULL_PRECISION)
    return (mean_state + moved).astype(jnp.bfloat16)

def offsets(neighbours, own_row, own_column, row_count, column_count):
    near_row = (neighbours // column_count - own_row + 1) % row_count - 1
    near_column = (neighbours % column_count - own_column + 2) % column_count - 2
    distance = (near_row * near_row + near_column * near_column).astype(jnp.float32)
    return (near_row, near_column, 1.0 / (1.0 + distance / 2.0))

def reference(initial_fields, encode_weight, send_weight, receive_weight, update_weight, norm_gain, decode_weight, edge_senders, halo_nodes, observed_perturbation, observed_values, region_neighbours):
    block = (jnp.arange(NODES, dtype=jnp.int32) // NODE_DEV)[:, None]
    left_pick = jnp.clip(edge_senders - NODE_DEV, 0, HALO - 1)
    right_pick = jnp.clip(edge_senders - NODE_DEV - HALO, 0, HALO - 1)
    left_node = (block - 1) % AREA_LONGITUDES * NODE_DEV + halo_nodes[0][block * HALO + left_pick]
    right_node = (block + 1) % AREA_LONGITUDES * NODE_DEV + halo_nodes[1][block * HALO + right_pick]
    own_node = block * NODE_DEV + jnp.minimum(edge_senders, NODE_DEV - 1)
    senders = jnp.where(edge_senders < NODE_DEV, own_node, jnp.where(edge_senders < NODE_DEV + HALO, left_node, right_node)).astype(jnp.int32)

    def predicted_replica(present_field):
        stream = wide_dot(present_field.T, encode_weight)
        for layer_index in range(LAYERS):
            rounded = stream.astype(jnp.bfloat16)
            sent = wide_dot(rounded, send_weight[layer_index]).astype(jnp.bfloat16)
            received = wide_dot(rounded, receive_weight[layer_index])
            messages = jnp.zeros_like(received)
            for slot_index in range(DEG):
                picked_rows = sent[senders[:, slot_index]].astype(jnp.float32)
                messages = messages + jax.nn.silu(picked_rows + received)
            normed = normalize(messages, norm_gain[layer_index]).astype(jnp.bfloat16)
            stream = stream + wide_dot(normed, update_weight[layer_index])
        field_change = wide_dot(stream.astype(jnp.bfloat16), decode_weight)
        return (present_field.astype(jnp.float32) + field_change.T).astype(jnp.bfloat16)
    predicted_fields = lax.map(predicted_replica, initial_fields)
    domain_pieces = predicted_fields.reshape(MEMBER_TOTAL, VERTEX_FEATURES, AREA_LONGITUDES, AREA_LATITUDES, AREA_VERTICES).transpose(3, 2, 0, 1, 4).reshape(AREA_TOTAL, MEMBER_TOTAL, VERTEX_FEATURES * AREA_VERTICES)

    def region_step(inputs):
        states, region, neighbours = inputs
        _, _, weights = offsets(neighbours, region // AREA_LONGITUDES, region % AREA_LONGITUDES, AREA_LATITUDES, AREA_LONGITUDES)
        chosen = jnp.concatenate([region[None], neighbours]).astype(jnp.int32)
        all_weights = jnp.concatenate([jnp.ones((1,), jnp.float32), weights])
        perturbation = observed_perturbation[chosen].astype(jnp.float32)
        values = observed_values[chosen].astype(jnp.float32)
        partial_grams = jnp.einsum('kio,kjo->kij', perturbation * values[:, 0][:, None, :], perturbation, precision=FULL_PRECISION)
        gram_matrix = jnp.einsum('k,kij->ij', all_weights, partial_grams, precision=FULL_PRECISION)
        partial_forcing = jnp.einsum('kio,ko->ki', perturbation, values[:, 0] * values[:, 1], precision=FULL_PRECISION)
        forcing = jnp.dot(all_weights, partial_forcing, precision=FULL_PRECISION)
        return analyse(states.astype(jnp.float32), gram_matrix, forcing)
    analysed = lax.map(region_step, (domain_pieces, jnp.arange(AREA_TOTAL, dtype=jnp.int32), region_neighbours))
    return analysed.reshape(AREA_LATITUDES, AREA_LONGITUDES, MEMBER_TOTAL, VERTEX_FEATURES, AREA_VERTICES).transpose(2, 3, 1, 0, 4).reshape(MEMBER_TOTAL, VERTEX_FEATURES, NODES)
```

```python
import functools

import jax
import jax.numpy as jnp
from jax import lax
from jax.experimental import pallas as pl
from jax.experimental.pallas import tpu as pltpu
from jax.sharding import PartitionSpec as P

ITERS_NS = 5
EPSILON = 1e-05
F32 = jnp.float32
BF16 = jnp.bfloat16
FULL_PRECISION = lax.Precision.HIGHEST
VMEM = pl.BlockSpec(memory_space=pltpu.VMEM)
SMEM = pl.BlockSpec(memory_space=pltpu.SMEM)
TAIL = 16


def dot(left, right):
    return jnp.dot(left, right, preferred_element_type=F32)


def dot_t(left, right):
    return lax.dot_general(left, right, (((1,), (1,)), ((), ())), preferred_element_type=F32)


def split(value):
    high = value.astype(BF16)
    return high, (value - high.astype(F32)).astype(BF16)


def call(kernel, shapes, inputs, specs=None, scratch=(), flops=0):
    return pl.pallas_call(
        kernel,
        out_shape=shapes,
        in_specs=specs or [VMEM] * len(inputs),
        out_specs=jax.tree.map(lambda _: VMEM, shapes),
        scratch_shapes=list(scratch),
        compiler_params=pltpu.CompilerParams(vmem_limit_bytes=40 * 1024 * 1024),
        cost_estimate=pl.CostEstimate(flops=flops, bytes_accessed=1 << 20, transcendentals=0),
    )(*inputs)


def gram_kernel(perturbation, values, lists, out):
    ensemble = perturbation.shape[1]
    members = perturbation[0]
    wide = values[0].astype(F32)
    high, low = split(members.astype(F32) * wide[0:1])
    gram = dot_t(high, members) + dot_t(low, members)
    high, low = split(jnp.broadcast_to(wide[0:1] * wide[1:2], (TAIL, wide.shape[1])))
    forcing = dot_t(high, members) + dot_t(low, members)
    high, low = split(forcing)
    row = lax.broadcasted_iota(jnp.int32, forcing.shape, 0)
    tail = jnp.where(row == 0, high.astype(F32), jnp.where(row == 1, low.astype(F32), lists[...].astype(F32)))
    out[:ensemble, :] = gram.astype(BF16)
    out[ensemble:, :] = tail.astype(BF16)


def paired(fields, pair):
    half = fields.shape[0] // 2
    return jnp.concatenate([fields[pair], fields[pair + half]], axis=0)


def pick_kernel(halo_count, fields, own, before, after, to_before, to_after, column, scratch):
    half = fields.shape[0] // 2
    nodes = fields.shape[2]
    rows = own.shape[0]
    ensemble = rows - TAIL
    wanted_before = before[ensemble:, :].astype(F32)[3:4]
    wanted_after = after[ensemble:, :].astype(F32)[2:3]
    node = lax.broadcasted_iota(jnp.int32, (nodes, wanted_before.shape[1]), 0).astype(F32)
    chosen = jnp.concatenate(
        [(node == wanted).astype(F32).T[:halo_count].astype(BF16) for wanted in (wanted_before, wanted_after)],
        axis=0,
    )
    for pair in range(half):
        picked = dot_t(chosen, paired(fields, pair))
        scratch[pl.ds(pair, 2 * halo_count, stride=half), :] = picked
    size = halo_count * half
    to_before[:size, :] = scratch[:size, :].astype(BF16)
    to_after[:size, :] = scratch[size:, :].astype(BF16)
    to_before[size:, :] = after[...]
    to_after[size:, :] = before[...]
    column[:rows, :] = before[...]
    column[rows : 2 * rows, :] = own[...]
    column[2 * rows :, :] = after[...]


def block_diagonal(weight):
    zero = jnp.zeros_like(weight)
    return jnp.concatenate(
        [jnp.concatenate([weight, zero], axis=1), jnp.concatenate([zero, weight], axis=1)], axis=0
    )


def halves(wide, nodes, half, hidden):
    return jnp.concatenate(
        [wide[:, :hidden].reshape(nodes, half, hidden), wide[:, hidden:].reshape(nodes, half, hidden)], axis=1
    )


def own_kernel(fields, encode, send, receive, rearranged, sent, received, scratch):
    half = fields.shape[0] // 2
    nodes = fields.shape[2]
    hidden = encode.shape[1]
    for pair in range(half):
        scratch[pl.ds(pair, nodes, stride=half), :] = paired(fields, pair).astype(F32).T
    both = block_diagonal(encode[...])
    send_half = send[0] * 0.5
    receive_half = receive[0] * 0.5
    step_nodes = 16
    size = step_nodes * half

    def step(index, carry):
        start = pl.multiple_of(index * size, size)
        rows = scratch[pl.ds(start, size), :].astype(BF16)
        rearranged[pl.ds(start, size), :] = rows
        stream = halves(dot(rows, both), step_nodes, half, hidden)
        rounded = stream.astype(BF16).reshape(step_nodes * 2 * half, hidden)
        shape = (step_nodes, 2 * half, hidden)
        at = pl.ds(index * step_nodes, step_nodes)
        sent[at] = dot(rounded, send_half).astype(BF16).reshape(shape)
        received[at] = dot(rounded, receive_half).reshape(shape)
        return carry

    lax.fori_loop(0, nodes // step_nodes, step, 0)


def message_kernel(
    halo_count,
    edges,
    rearranged,
    sent,
    received,
    from_before,
    from_after,
    encode,
    send,
    update,
    gain,
    decode,
    out,
    extended,
    normed,
):
    nodes, members, hidden = sent.shape
    half = members // 2
    degree = edges.shape[0] // nodes
    regions = out.shape[0]
    channels = decode.shape[1]
    both = block_diagonal(encode[...])
    send_half = send[0] * 0.5
    extended[:nodes] = sent[...]
    for side, source in enumerate((from_before, from_after)):
        stream = halves(dot(source[: halo_count * half, :], both), halo_count, half, hidden)
        rounded = stream.astype(BF16).reshape(halo_count * members, hidden)
        start = nodes + side * halo_count
        extended[start : start + halo_count] = (
            dot(rounded, send_half).astype(BF16).reshape(halo_count, members, hidden)
        )
    zero = jnp.zeros_like(decode[...])
    decode_even = jnp.concatenate([decode[...], zero], axis=1)
    decode_odd = jnp.concatenate([zero, decode[...]], axis=1)
    step_nodes = 8
    per_region = nodes // regions // step_nodes
    gains = gain[...].astype(F32)

    def step(index, carry):
        base = index * step_nodes
        for offset in range(step_nodes):
            node = base + offset
            here = received[node]
            messages = jnp.zeros_like(here)
            for slot in range(degree):
                moved = extended[edges[node * degree + slot]].astype(F32) + here
                messages = messages + (moved + moved * jnp.tanh(moved))
            mean_square = jnp.mean(messages * messages, axis=-1, keepdims=True)
            scaled = messages * lax.rsqrt(mean_square + EPSILON) * gains
            normed[offset * members : (offset + 1) * members, :] = scaled.astype(BF16)
        start = pl.multiple_of(base * half, step_nodes * half)
        fields = rearranged[pl.ds(start, step_nodes * half), :]
        stream = halves(dot(fields, both), step_nodes, half, hidden).reshape(step_nodes * members, hidden)
        stream = stream + dot(normed[...], update[0])
        final = stream.astype(BF16).reshape(step_nodes // 2, 2, members, hidden)
        rows = step_nodes // 2 * members
        change = dot(final[:, 0].reshape(rows, hidden), decode_even) + dot(
            final[:, 1].reshape(rows, hidden), decode_odd
        )
        wide = fields.astype(F32).reshape(step_nodes // 2, 2, half, 2 * channels)
        even, odd = wide[:, 0], wide[:, 1]
        low = lax.broadcasted_iota(jnp.int32, even.shape, 2) < channels
        first = jnp.where(low, even, pltpu.roll(odd, channels, 2))
        second = jnp.where(low, pltpu.roll(even, channels, 2), odd)
        initial = jnp.concatenate([first, second], axis=1)
        forecast = (initial + change.reshape(initial.shape)).astype(BF16)
        region = index // per_region
        within = index % per_region
        width = 2 * channels
        for pair in range(step_nodes // 2):
            lane = pl.multiple_of((within * (step_nodes // 2) + pair) * width, width)
            out[region, :, pl.ds(lane, width)] = forecast[pair]
        return carry

    lax.fori_loop(0, nodes // step_nodes, step, 0)


def weights_kernel(slot_weight, own, before, after, from_before, from_after, up, down, out):
    rows, ensemble = own.shape
    near = from_before.shape[0] - rows
    total = None
    sources = [(up, 0), (up, rows), (up, 2 * rows), (before, 0), (own, 0), (after, 0)]
    sources += [(down, 0), (down, rows), (down, 2 * rows), (from_before, near), (from_after, near)]
    for slot, (source, start) in enumerate(sources):
        part = slot_weight[slot] * source[start : start + rows, :].astype(F32)
        total = part if total is None else total + part
    identity = (
        lax.broadcasted_iota(jnp.int32, (ensemble, ensemble), 0)
        == lax.broadcasted_iota(jnp.int32, (ensemble, ensemble), 1)
    ).astype(F32)
    full = functools.partial(jnp.dot, precision=FULL_PRECISION, preferred_element_type=F32)
    system = identity + total[:ensemble] / (ensemble - 1)
    squares = jnp.sum(jnp.sum(system * system, axis=1, keepdims=True), axis=0, keepdims=True)
    scaling = jnp.sqrt(squares)
    iterate = system / scaling
    correction = 1.5 * identity - 0.5 * iterate
    inverse = correction
    for _ in range(ITERS_NS - 1):
        iterate = full(iterate, correction)
        correction = 1.5 * identity - 0.5 * full(inverse, iterate)
        inverse = full(correction, inverse)
    tail = total[ensemble:]
    forcing = jnp.broadcast_to(tail[0:1] + tail[1:2], (8, ensemble))
    mean_weights = full(full(forcing, inverse), inverse)[0:1] / (scaling * (ensemble - 1))
    transform = inverse / jnp.sqrt(scaling) + mean_weights
    rest = (1.0 - jnp.sum(transform, axis=1, keepdims=True)) / ensemble
    high, low = split(transform + rest)
    out[:, :ensemble] = high
    out[:, ensemble:] = low


def analysis_kernel(weights, states, out):
    groups, members, width = states.shape
    ensemble = groups * members
    step_width = 256

    def step(index, carry):
        at = pl.ds(pl.multiple_of(index * step_width, step_width), step_width)
        columns = states[:, :, at].reshape(ensemble, step_width)
        analysed = dot(weights[...], jnp.concatenate([columns, columns], axis=0))
        out[:, :, at] = analysed.astype(BF16).reshape(groups, members, step_width)
        return carry

    lax.fori_loop(0, width // step_width, step, 0, unroll=True)


def output_kernel(analysed, out, scratch):
    regions, members, width = analysed.shape
    half = members // 2
    channels = out.shape[1]
    nodes = out.shape[2]
    low = lax.broadcasted_iota(jnp.int32, (half, 2 * channels), 1) < channels
    per_region = nodes // regions // 2
    for region in range(regions):
        for pair in range(per_region):
            block = analysed[region, :, pair * 2 * channels : (pair + 1) * 2 * channels].astype(F32)
            first, second = block[:half], block[half:]
            node = region * per_region * 2 + pair * 2
            scratch[node * half : (node + 1) * half, :] = jnp.where(low, first, pltpu.roll(second, channels, 1))
            scratch[(node + 1) * half : (node + 2) * half, :] = jnp.where(
                low, pltpu.roll(first, channels, 1), second
            )
    for pair in range(half):
        block = scratch[pl.ds(pair, nodes, stride=half), :].T.astype(BF16)
        out[pair] = block[:channels]
        out[pair + half] = block[channels:]


def slot_weights(neighbours, own_row, own_column, row_count, column_count):
    near_row = (neighbours // column_count - own_row + 1) % row_count - 1
    near_column = (neighbours % column_count - own_column + 2) % column_count - 2
    distance = (near_row * near_row + near_column * near_column).astype(F32)
    weights = 1.0 / (1.0 + distance / 2.0)
    slot = jnp.where(
        near_column == -2, 9, jnp.where(near_column == 2, 10, (near_row + 1) * 3 + near_column + 1)
    )
    slot_range = jnp.arange(11, dtype=jnp.int32)
    chosen = (slot[:, None] == slot_range[None, :]).astype(F32)
    return jnp.sum(weights[:, None] * chosen, axis=0) + (slot_range == 4).astype(F32)


def ring(value, axis, shift):
    count = lax.axis_size(axis)
    return lax.ppermute(value, axis, [(i, (i + shift) % count) for i in range(count)])


def body(
    initial_fields,
    encode_weight,
    send_weight,
    receive_weight,
    update_weight,
    norm_gain,
    decode_weight,
    edge_senders,
    halo_nodes,
    observed_perturbation,
    observed_values,
    region_neighbours,
):
    members, channels, nodes = initial_fields.shape
    hidden = encode_weight.shape[1]
    half = members // 2
    halo_count = halo_nodes.shape[1]
    ensemble = observed_perturbation.shape[1]
    groups = lax.axis_size("member")
    rows = ensemble + TAIL
    struct = jax.ShapeDtypeStruct
    lists = jnp.pad(halo_nodes.astype(BF16), ((2, TAIL - 4), (0, ensemble - halo_count)))
    own = call(
        gram_kernel, struct((rows, ensemble), BF16), (observed_perturbation, observed_values, lists), flops=1 << 24
    )
    before = ring(own, "space", 1)
    after = ring(own, "space", -1)
    rearranged, sent, received = call(
        own_kernel,
        (
            struct((nodes * half, 2 * channels), BF16),
            struct((nodes, members, hidden), BF16),
            struct((nodes, members, hidden), F32),
        ),
        (initial_fields, encode_weight, send_weight, receive_weight),
        scratch=[pltpu.VMEM((nodes * half, 2 * channels), F32)],
        flops=1 << 30,
    )
    size = halo_count * half
    to_before, to_after, column = call(
        functools.partial(pick_kernel, halo_count),
        (
            struct((size + rows, 2 * channels), BF16),
            struct((size + rows, 2 * channels), BF16),
            struct((3 * rows, ensemble), BF16),
        ),
        (initial_fields, own, before, after),
        scratch=[pltpu.VMEM((2 * size, 2 * channels), F32)],
        flops=1 << 27,
    )
    from_before = ring(to_after, "space", 1)
    from_after = ring(to_before, "space", -1)
    up = ring(column, "member", 1)
    down = ring(column, "member", -1)
    width = nodes // groups * channels
    predicted = call(
        functools.partial(message_kernel, halo_count),
        struct((groups, members, width), BF16),
        (
            edge_senders.reshape(-1),
            rearranged,
            sent,
            received,
            from_before,
            from_after,
            encode_weight,
            send_weight,
            update_weight,
            norm_gain,
            decode_weight,
        ),
        specs=[SMEM] + [VMEM] * 10,
        scratch=[
            pltpu.VMEM((nodes + 2 * halo_count, members, hidden), BF16),
            pltpu.VMEM((8 * members, hidden), BF16),
        ],
        flops=1 << 32,
    )
    states = lax.all_to_all(predicted, "member", split_axis=0, concat_axis=0, tiled=True)
    slot_weight = slot_weights(
        region_neighbours[0],
        lax.axis_index("member"),
        lax.axis_index("space"),
        lax.axis_size("member"),
        lax.axis_size("space"),
    )
    weights = call(
        weights_kernel,
        struct((ensemble, 2 * ensemble), BF16),
        (slot_weight, own, before, after, from_before, from_after, up, down),
        specs=[SMEM] + [VMEM] * 7,
        flops=1 << 30,
    )
    analysed = call(analysis_kernel, struct((groups, members, width), BF16), (weights, states), flops=1 << 28)
    returned = lax.all_to_all(analysed, "member", split_axis=0, concat_axis=0, tiled=True)
    return call(
        output_kernel,
        struct((members, channels, nodes), BF16),
        (returned,),
        scratch=[pltpu.VMEM((nodes * half, 2 * channels), F32)],
        flops=1 << 20,
    )


def solution(mesh):
    placed = (
        P("member", None, "space"),
        P(),
        P(),
        P(),
        P(),
        P(),
        P(),
        P("space", None),
        P(None, "space"),
        P(("member", "space"), None, None),
        P(("member", "space"), None, None),
        P(("member", "space"), None),
    )
    return jax.shard_map(
        body, mesh=mesh, in_specs=placed, out_specs=P("member", None, "space"), check_vma=False
    )
```

```python
import functools

import jax
import jax.numpy as jnp
from jax import lax
from jax.experimental import pallas as pl
from jax.experimental.pallas import tpu as pltpu
from jax.sharding import PartitionSpec as P

ITERS_NS = 5
EPSILON = 1e-05
F32 = jnp.float32
BF16 = jnp.bfloat16
FULL_PRECISION = lax.Precision.HIGHEST
VMEM = pl.BlockSpec(memory_space=pltpu.VMEM)
SMEM = pl.BlockSpec(memory_space=pltpu.SMEM)
TAIL = 16
NOWHERE = -1048576.0
BATCH = 8
HBM = pl.BlockSpec(memory_space=pltpu.HBM)


def dot(left, right):
    return jnp.dot(left, right, preferred_element_type=F32)


def dot_t(left, right):
    return lax.dot_general(left, right, (((1,), (1,)), ((), ())), preferred_element_type=F32)


def split(value):
    high = value.astype(BF16)
    return high, (value - high.astype(F32)).astype(BF16)


def placed_in(space, *values):
    return tuple(pltpu.with_memory_space_constraint(value, space) for value in values)


def call(kernel, shapes, inputs, specs=None, outs=None, scratch=(), flops=0, aliases=None):
    return pl.pallas_call(
        kernel,
        out_shape=shapes,
        in_specs=specs or [VMEM] * len(inputs),
        out_specs=outs or jax.tree.map(lambda _: VMEM, shapes),
        scratch_shapes=list(scratch),
        input_output_aliases=aliases or {},
        compiler_params=pltpu.CompilerParams(vmem_limit_bytes=16 * 1024 * 1024),
        cost_estimate=pl.CostEstimate(flops=flops, bytes_accessed=1 << 20, transcendentals=0),
    )(*inputs)


def gram_kernel(perturbation, values, halo_nodes, out, held, held_values, held_lists, sems):
    copies = [
        pltpu.make_async_copy(source, target, sems.at[index])
        for index, (source, target) in enumerate(
            ((perturbation, held), (values, held_values), (halo_nodes, held_lists))
        )
    ]
    for copy in copies:
        copy.start()
    for copy in copies:
        copy.wait()
    ensemble = held.shape[1]
    members = held[0]
    wide = held_values[0].astype(F32)
    high, low = split(members.astype(F32) * wide[0:1])
    gram = dot_t(high, members) + dot_t(low, members)
    high, low = split(jnp.broadcast_to(wide[0:1] * wide[1:2], (TAIL, wide.shape[1])))
    forcing = dot_t(high, members) + dot_t(low, members)
    high, low = split(forcing)
    lists = held_lists[...].astype(F32)
    lists = jnp.concatenate([lists, jnp.zeros((2, ensemble - lists.shape[1]), F32)], axis=1)
    row = lax.broadcasted_iota(jnp.int32, forcing.shape, 0)
    tail = jnp.where(row == 0, high.astype(F32), low.astype(F32))
    tail = jnp.where(row == 2, lists[0:1], jnp.where(row == 3, lists[1:2], tail))
    out[:ensemble, :] = gram.astype(BF16)
    out[ensemble:, :] = tail.astype(BF16)


def paired(fields, pair):
    half = fields.shape[0] // 2
    return jnp.concatenate([fields[pair], fields[pair + half]], axis=0)


def pick_kernel(halo_count, columns, before, after, up, down, to_before, to_after, scratch):
    half, nodes, _ = columns.shape
    rows = before.shape[0]
    ensemble = rows - TAIL
    wanted_before = before[ensemble:, :].astype(F32)[3:4]
    wanted_after = after[ensemble:, :].astype(F32)[2:3]
    node = lax.broadcasted_iota(jnp.int32, (nodes, wanted_before.shape[1]), 0).astype(F32)
    chosen = jnp.concatenate(
        [(node == wanted).astype(F32).T[:halo_count].astype(BF16) for wanted in (wanted_before, wanted_after)],
        axis=0,
    )
    for pair in range(half):
        picked = dot(chosen, columns[pair])
        scratch[pl.ds(pair, 2 * halo_count, stride=half), :] = picked
    size = halo_count * half
    to_before[:size, :] = scratch[:size, :].astype(BF16)
    to_after[:size, :] = scratch[size:, :].astype(BF16)
    for target, beyond in ((to_before, after), (to_after, before)):
        for index, source in enumerate((beyond, up, down)):
            target[size + index * rows : size + (index + 1) * rows, :] = source[...]


def block_diagonal(weight):
    zero = jnp.zeros_like(weight)
    return jnp.concatenate(
        [jnp.concatenate([weight, zero], axis=1), jnp.concatenate([zero, weight], axis=1)], axis=0
    )


def halves(wide, nodes, half, hidden):
    return jnp.concatenate(
        [wide[:, :hidden].reshape(nodes, half, hidden), wide[:, hidden:].reshape(nodes, half, hidden)], axis=1
    )


def own_kernel(partners, fields, encode, send, receive, columns, rearranged, sent, received, held, held_encode, held_send, held_receive, scratch, sems):
    half = fields.shape[0] // 2
    nodes = fields.shape[2]
    hidden = encode.shape[1]
    copies = [
        pltpu.make_async_copy(source, target, sems.at[index])
        for index, (source, target) in enumerate(
            ((fields, held), (encode, held_encode), (send, held_send), (receive, held_receive))
        )
    ]
    for copy in copies:
        copy.start()
    for copy in copies:
        copy.wait()
    for pair in range(half):
        column = paired(held, pair).astype(F32).T
        scratch[pl.ds(pair, nodes, stride=half), :] = column
        columns[pair] = column.astype(BF16)
    both = block_diagonal(held_encode[...])
    send_half = held_send[0] * 0.5
    receive_half = held_receive[0] * 0.5
    sent[nodes] = jnp.full(sent.shape[1:], NOWHERE, BF16)
    step_nodes = 32
    size = step_nodes * half
    for index in range(nodes // step_nodes):
        rows = scratch[index * size : (index + 1) * size, :].astype(BF16)
        rearranged[index * size : (index + 1) * size, :] = rows
        stream = halves(dot(rows, both), step_nodes, half, hidden)
        rounded = stream.astype(BF16).reshape(step_nodes * 2 * half, hidden)
        shape = (step_nodes, 2 * half, hidden)
        at = slice(index * step_nodes, (index + 1) * step_nodes)
        sent[at] = dot(rounded, send_half).astype(BF16).reshape(shape)
        received[at] = dot(rounded, receive_half).reshape(shape)


def activated(sender, here):
    moved = sender.astype(F32) + here
    return moved + moved * jnp.tanh(moved)


def own_message_kernel(halo_total, edges, sent, received, messages, halo_edges, halo_edge_count):
    nodes, members, hidden = received.shape
    degree = edges.shape[0]
    group = 4

    def step(index, count):
        for offset in range(group):
            node = index * group + offset
            here = received[node]
            total = None
            for slot in range(degree):
                sender = edges[slot, node]
                value = activated(sent[jnp.minimum(sender, nodes)], here)
                total = value if total is None else total + value
                halo_edges[count] = node * halo_total + sender - nodes
                count = count + jnp.where(sender < nodes, 0, 1)
            messages[node] = total
        return count

    count = lax.fori_loop(0, nodes // group, step, 0)
    for index in range(BATCH):
        halo_edges[count + index] = nodes * halo_total
    halo_edge_count[0] = count
    messages[nodes] = jnp.zeros((members, hidden), F32)


def message_kernel(
    halo_count,
    partners,
    halo_edges,
    halo_edge_count,
    rearranged,
    received,
    started,
    from_before,
    from_after,
    encode,
    send,
    update,
    gain,
    decode,
    *outputs,
):
    *outs, messages, extended = outputs
    nodes, members, hidden = received.shape
    half = members // 2
    regions = len(outs)
    channels = decode.shape[0]
    both = block_diagonal(encode[...])
    send_half = send[0] * 0.5
    for side, source in enumerate((from_before, from_after)):
        stream = halves(dot(source[: halo_count * half, :], both), halo_count, half, hidden)
        rounded = stream.astype(BF16).reshape(halo_count * members, hidden)
        extended[side * halo_count : (side + 1) * halo_count] = (
            dot(rounded, send_half).astype(BF16).reshape(halo_count, members, hidden)
        )

    def batch(index, carry):
        found = []
        for offset in range(BATCH):
            code = halo_edges[index * BATCH + offset]
            node = code // (2 * halo_count)
            here = received[jnp.minimum(node, nodes - 1)]
            found.append((node, activated(extended[code % (2 * halo_count)], here)))
        for node, value in found:
            messages[node] = messages[node] + value
        return carry

    lax.fori_loop(0, (halo_edge_count[0] + BATCH - 1) // BATCH, batch, 0)
    zero = jnp.zeros_like(decode[...])
    decode_even = jnp.concatenate([decode[...], zero], axis=0)
    decode_odd = jnp.concatenate([zero, decode[...]], axis=0)
    gains = gain[...].astype(F32)
    chunk = nodes // regions
    pairs = chunk // 2
    width = 2 * channels
    average = jnp.full((hidden, width), 1.0 / hidden, BF16)
    low = lax.broadcasted_iota(jnp.int32, (pairs, half, width), 2) < channels
    for index, out in enumerate(outs):
        base = partners[index] * chunk
        fields = rearranged[pl.ds(pl.multiple_of(base * half, chunk * half), chunk * half), :]
        stream = halves(dot(fields, both), chunk, half, hidden).reshape(chunk * members, hidden)
        message = messages[pl.ds(base, chunk)].reshape(chunk * members, hidden)
        mean_square = dot((message * message).astype(BF16), average)
        scale = lax.rsqrt(mean_square + EPSILON)
        scaled = message * jnp.concatenate([scale] * (hidden // width), axis=1) * gains
        stream = stream + dot(scaled.astype(BF16), update[0])
        final = stream.astype(BF16).reshape(pairs, 2, members, hidden)
        rows = pairs * members
        change = dot_t(final[:, 0].reshape(rows, hidden), decode_even) + dot_t(
            final[:, 1].reshape(rows, hidden), decode_odd
        )
        wide = fields.astype(F32).reshape(pairs, 2, half, width)
        even, odd = wide[:, 0], wide[:, 1]
        first = jnp.where(low, even, pltpu.roll(odd, channels, 2))
        second = jnp.where(low, pltpu.roll(even, channels, 2), odd)
        initial = jnp.concatenate([first, second], axis=1)
        forecast = (initial + change.reshape(initial.shape)).astype(BF16)
        for pair in range(pairs):
            out[:, pair * width : (pair + 1) * width] = forecast[pair]


def weights_kernel(partners, neighbours, own, before, after, up, down, from_before, from_after, out):
    rows, ensemble = own.shape
    first = from_before.shape[0] - 3 * rows
    row_count = (partners.shape[0] - 2) // 2
    column_count = partners[partners.shape[0] - 1]
    own_row, own_column = partners[0], partners[partners.shape[0] - 2]
    offsets = []
    for index in range(neighbours.shape[1]):
        region = neighbours[0, index]
        near_row = (region // column_count - own_row + 1 + row_count) % row_count - 1
        near_column = (region % column_count - own_column + 2 + column_count) % column_count - 2
        offsets.append((near_row, near_column))
    sources = {(0, -1): (before, 0), (0, 1): (after, 0), (-1, 0): (up, 0), (1, 0): (down, 0)}
    for column, source in ((-1, from_before), (1, from_after)):
        for index, place in enumerate(((0, 2 * column), (-1, column), (1, column))):
            sources[place] = (source, first + index * rows)
    total = own[...].astype(F32)
    for place, (source, start) in sources.items():
        weight = 0.0
        for near_row, near_column in offsets:
            here = jnp.logical_and(near_row == place[0], near_column == place[1])
            weight = weight + jnp.where(here, 1.0 / (1.0 + (place[0] ** 2 + place[1] ** 2) / 2.0), 0.0)
        total = total + weight * source[start : start + rows, :].astype(F32)
    identity = (
        lax.broadcasted_iota(jnp.int32, (ensemble, ensemble), 0)
        == lax.broadcasted_iota(jnp.int32, (ensemble, ensemble), 1)
    ).astype(F32)
    full = functools.partial(jnp.dot, precision=FULL_PRECISION, preferred_element_type=F32)
    system = identity + total[:ensemble] / (ensemble - 1)
    squares = jnp.sum(jnp.sum(system * system, axis=1, keepdims=True), axis=0, keepdims=True)
    scaling = jnp.sqrt(squares)
    iterate = system / scaling
    correction = 1.5 * identity - 0.5 * iterate
    inverse = correction
    for _ in range(ITERS_NS - 1):
        iterate = full(iterate, correction)
        correction = 1.5 * identity - 0.5 * full(inverse, iterate)
        inverse = full(correction, inverse)
    tail = total[ensemble:]
    forcing = jnp.broadcast_to(tail[0:1] + tail[1:2], (8, ensemble))
    mean_weights = full(full(forcing, inverse), inverse)[0:1] / (scaling * (ensemble - 1))
    transform = inverse / jnp.sqrt(scaling) + mean_weights
    rest = (1.0 - jnp.sum(transform, axis=1, keepdims=True)) / ensemble
    members = ensemble // row_count
    to_rows = lax.broadcasted_iota(jnp.int32, (ensemble, ensemble), 0)
    to_columns = lax.broadcasted_iota(jnp.int32, (ensemble, ensemble), 1)
    wanted_rows, wanted_columns = to_rows % members, to_columns % members
    for index in range(row_count):
        target, origin = partners[index] * members, partners[row_count + index] * members
        wanted_rows = wanted_rows + jnp.where(to_rows // members == index, target, 0)
        wanted_columns = wanted_columns + jnp.where(to_columns // members == index, origin, 0)
    by_row = (to_columns == wanted_rows).astype(F32).astype(BF16)
    by_column = (to_rows == wanted_columns).astype(F32).astype(BF16)
    for index, part in enumerate(split(transform + rest)):
        moved = dot(dot(by_row, part).astype(BF16), by_column)
        out[:, index * ensemble : (index + 1) * ensemble] = moved.astype(BF16)


def analysis_kernel(weights, *refs):
    count = len(refs) // 2
    pieces, outs = refs[:count], refs[count:]
    members, width = pieces[0].shape
    step_width = 512
    for start in range(0, width, step_width):
        columns = [piece[:, start : start + step_width] for piece in pieces]
        analysed = dot(weights[...], jnp.concatenate(columns * 2, axis=0)).astype(BF16)
        for index, out in enumerate(outs):
            out[:, start : start + step_width] = analysed[index * members : (index + 1) * members]


def output_kernel(partners, *refs):
    *pieces, out, held, scratch = refs
    count = len(pieces)
    members, channels, nodes = out.shape
    half = members // 2
    low = lax.broadcasted_iota(jnp.int32, (half, 2 * channels), 1) < channels
    chunk = nodes // count
    for index, piece in enumerate(pieces):
        held[partners[count + index]] = piece[...]
    for region in range(count):
        for pair in range(chunk // 2):
            block = held[region, :, pair * 2 * channels : (pair + 1) * 2 * channels].astype(F32)
            first, second = block[:half], block[half:]
            row = (region * chunk + 2 * pair) * half
            scratch[row : row + half, :] = jnp.where(low, first, pltpu.roll(second, channels, 1))
            scratch[row + half : row + 2 * half, :] = jnp.where(low, pltpu.roll(first, channels, 1), second)
    for pair in range(half):
        block = scratch[pl.ds(pair, nodes, stride=half), :].T.astype(BF16)
        out[pair] = block[:channels]
        out[pair + half] = block[channels:]


def ring(value, axis, shift):
    count = lax.axis_size(axis)
    return lax.ppermute(value, axis, [(i, (i + shift) % count) for i in range(count)])


def partner_exchange(axis):
    count = lax.axis_size(axis)
    own = lax.axis_index(axis)
    steps = jnp.arange(count, dtype=jnp.int32)
    paired_up = count & (count - 1) == 0
    if paired_up:
        targets = origins = own ^ steps
    else:
        targets, origins = (own + steps) % count, (own - steps) % count

    def exchange(pieces):
        return [pieces[0]] + [
            lax.ppermute(
                piece, axis, [(i, i ^ step if paired_up else (i + step) % count) for i in range(count)]
            )
            for step, piece in enumerate(pieces)
            if step
        ]

    place = jnp.stack([lax.axis_index("space"), jnp.int32(lax.axis_size("space"))])
    return jnp.concatenate([targets, origins, place]), exchange


def body(
    initial_fields,
    encode_weight,
    send_weight,
    receive_weight,
    update_weight,
    norm_gain,
    decode_weight,
    edge_senders,
    halo_nodes,
    observed_perturbation,
    observed_values,
    region_neighbours,
):
    members, channels, nodes = initial_fields.shape
    hidden = encode_weight.shape[1]
    half = members // 2
    halo_count = halo_nodes.shape[1]
    ensemble = observed_perturbation.shape[1]
    groups = lax.axis_size("member")
    rows = ensemble + TAIL
    struct = jax.ShapeDtypeStruct
    own = call(
        gram_kernel,
        struct((rows, ensemble), BF16),
        placed_in(pltpu.HBM, observed_perturbation, observed_values, halo_nodes),
        specs=[HBM] * 3,
        scratch=[
            pltpu.VMEM(observed_perturbation.shape, BF16),
            pltpu.VMEM(observed_values.shape, BF16),
            pltpu.VMEM(halo_nodes.shape, jnp.int32),
            pltpu.SemaphoreType.DMA((3,)),
        ],
        flops=1 << 24,
    )
    before = ring(own, "space", 1)
    after = ring(own, "space", -1)
    up = ring(own, "member", 1)
    down = ring(own, "member", -1)
    partners, exchange = partner_exchange("member")
    columns, rearranged, sent, received = call(
        own_kernel,
        (
            struct((half, nodes, 2 * channels), BF16),
            struct((nodes * half, 2 * channels), BF16),
            pltpu.VMEM((nodes + 1, members, hidden), BF16),
            pltpu.VMEM((nodes, members, hidden), F32),
        ),
        (partners, *placed_in(pltpu.HBM, initial_fields, encode_weight, send_weight, receive_weight)),
        specs=[SMEM] + [HBM] * 4,
        scratch=[
            pltpu.VMEM(initial_fields.shape, BF16),
            pltpu.VMEM(encode_weight.shape, BF16),
            pltpu.VMEM(send_weight.shape, BF16),
            pltpu.VMEM(receive_weight.shape, BF16),
            pltpu.VMEM((nodes * half, 2 * channels), F32),
            pltpu.SemaphoreType.DMA((4,)),
        ],
        flops=1 << 30,
    )
    size = halo_count * half
    to_before, to_after = call(
        functools.partial(pick_kernel, halo_count),
        (struct((size + 3 * rows, 2 * channels), BF16),) * 2,
        (columns, before, after, up, down),
        scratch=[pltpu.VMEM((2 * size, 2 * channels), F32)],
        flops=1 << 27,
    )
    from_before = ring(to_after, "space", 1)
    from_after = ring(to_before, "space", -1)
    edges = edge_senders.T
    started, halo_edges, halo_edge_count = call(
        functools.partial(own_message_kernel, 2 * halo_count),
        (
            pltpu.VMEM((nodes + 1, members, hidden), F32),
            struct((edges.size + BATCH,), jnp.int32),
            struct((1,), jnp.int32),
        ),
        (edges, *placed_in(pltpu.VMEM, sent, received)),
        specs=[SMEM, VMEM, VMEM],
        outs=(VMEM, SMEM, SMEM),
        flops=1 << 31,
    )
    width = nodes // groups * channels
    piece = struct((members, width), BF16)
    *predicted, _ = call(
        functools.partial(message_kernel, halo_count),
        (piece,) * groups + (struct(started.shape, F32),),
        (
            partners,
            halo_edges,
            halo_edge_count,
            rearranged,
            *placed_in(pltpu.VMEM, received, started),
            from_before,
            from_after,
            encode_weight,
            send_weight,
            update_weight,
            norm_gain,
            decode_weight.T,
        ),
        specs=[SMEM] * 3 + [VMEM] * 10,
        scratch=[pltpu.VMEM((2 * halo_count, members, hidden), BF16)],
        flops=1 << 32,
        aliases={5: groups},
    )
    states = exchange(predicted)
    weights = call(
        weights_kernel,
        struct((ensemble, 2 * ensemble), BF16),
        (partners, region_neighbours, own, before, after, up, down, from_before, from_after),
        specs=[SMEM] * 2 + [VMEM] * 7,
        flops=1 << 30,
    )
    analysed = call(
        analysis_kernel,
        (piece,) * groups,
        (weights, *states),
        flops=1 << 28,
    )
    returned = exchange(analysed)
    return call(
        output_kernel,
        struct((members, channels, nodes), BF16),
        (partners, *returned),
        specs=[SMEM] + [VMEM] * groups,
        scratch=[
            pltpu.VMEM((groups, members, width), BF16),
            pltpu.VMEM((nodes * half, 2 * channels), F32),
        ],
        flops=1 << 20,
    )


def solution(mesh):
    placed = (
        P("member", None, "space"),
        P(),
        P(),
        P(),
        P(),
        P(),
        P(),
        P("space", None),
        P(None, "space"),
        P(("member", "space"), None, None),
        P(("member", "space"), None, None),
        P(("member", "space"), None),
    )
    return jax.shard_map(
        body, mesh=mesh, in_specs=placed, out_specs=P("member", None, "space"), check_vma=False
    )
```

```python
import functools

import jax
import jax.numpy as jnp
from jax import lax
from jax.experimental import pallas as pl
from jax.experimental.pallas import tpu as pltpu
from jax.sharding import PartitionSpec as P

ITERS_NS = 5
EPSILON = 1e-05
F32 = jnp.float32
BF16 = jnp.bfloat16
FULL_PRECISION = lax.Precision.HIGHEST
VMEM = pl.BlockSpec(memory_space=pltpu.VMEM)
SMEM = pl.BlockSpec(memory_space=pltpu.SMEM)
TAIL = 16
NOWHERE = -1048576.0
OUTPUT_STEP = 4
BATCH = 16
HBM = pl.BlockSpec(memory_space=pltpu.HBM)
ANY = pl.BlockSpec(memory_space=pl.ANY)


def dot(left, right):
    return jnp.dot(left, right, preferred_element_type=F32)


def dot_t(left, right):
    return lax.dot_general(left, right, (((1,), (1,)), ((), ())), preferred_element_type=F32)


def split(value):
    high = value.astype(BF16)
    return high, (value - high.astype(F32)).astype(BF16)


def placed_in(space, *values):
    return tuple(pltpu.with_memory_space_constraint(value, space) for value in values)


def call(kernel, shapes, inputs, specs=None, outs=None, scratch=(), flops=0, aliases=None):
    return pl.pallas_call(
        kernel,
        out_shape=shapes,
        in_specs=specs or [VMEM] * len(inputs),
        out_specs=outs or jax.tree.map(lambda _: VMEM, shapes),
        scratch_shapes=list(scratch),
        input_output_aliases=aliases or {},
        compiler_params=pltpu.CompilerParams(vmem_limit_bytes=16 * 1024 * 1024),
        cost_estimate=pl.CostEstimate(flops=flops, bytes_accessed=1 << 20, transcendentals=0),
    )(*inputs)


def start_copies(sems, *ends):
    copies = [
        pltpu.make_async_copy(source, target, sems.at[index]) for index, (source, target) in enumerate(ends)
    ]
    for copy in copies:
        copy.start()
    return copies


def gram_kernel(perturbation, values, halo_nodes, fields, encode, send, receive, out, *refs):
    *near, held, held_values, held_lists, sems = refs
    copies = start_copies(
        sems,
        (perturbation, held),
        (values, held_values),
        (halo_nodes, held_lists),
        *zip((fields, encode, send, receive), near),
    )
    for copy in copies[:3]:
        copy.wait()
    ensemble = held.shape[1]
    members = held[0]
    wide = held_values[0].astype(F32)
    high, low = split(members.astype(F32) * wide[0:1])
    gram = dot_t(high, members) + dot_t(low, members)
    high, low = split(jnp.broadcast_to(wide[0:1] * wide[1:2], (TAIL, wide.shape[1])))
    forcing = dot_t(high, members) + dot_t(low, members)
    high, low = split(forcing)
    lists = held_lists[...].astype(F32)
    lists = jnp.concatenate([lists, jnp.zeros((2, ensemble - lists.shape[1]), F32)], axis=1)
    row = lax.broadcasted_iota(jnp.int32, forcing.shape, 0)
    tail = jnp.where(row == 0, high.astype(F32), low.astype(F32))
    tail = jnp.where(row == 2, lists[0:1], jnp.where(row == 3, lists[1:2], tail))
    out[:ensemble, :] = gram.astype(BF16)
    out[ensemble:, :] = tail.astype(BF16)
    for copy in copies[3:]:
        copy.wait()


def paired(fields, pair):
    half = fields.shape[0] // 2
    return jnp.concatenate([fields[pair], fields[pair + half]], axis=0)


def pick_kernel(halo_count, columns, own, before, after, to_before, to_after, column, scratch):
    half, nodes, _ = columns.shape
    rows = before.shape[0]
    ensemble = rows - TAIL
    wanted_before = before[ensemble:, :].astype(F32)[3:4]
    wanted_after = after[ensemble:, :].astype(F32)[2:3]
    node = lax.broadcasted_iota(jnp.int32, (nodes, wanted_before.shape[1]), 0).astype(F32)
    chosen = jnp.concatenate(
        [(node == wanted).astype(F32).T[:halo_count].astype(BF16) for wanted in (wanted_before, wanted_after)],
        axis=0,
    )
    for pair in range(half):
        picked = dot(chosen, columns[pair])
        scratch[pl.ds(pair, 2 * halo_count, stride=half), :] = picked
    size = halo_count * half
    to_before[:size, :] = scratch[:size, :].astype(BF16)
    to_after[:size, :] = scratch[size:, :].astype(BF16)
    to_before[size:, :] = after[...]
    to_after[size:, :] = before[...]
    for index, source in enumerate((before, own, after)):
        column[index * rows : (index + 1) * rows, :] = source[...]


def block_diagonal(weight):
    zero = jnp.zeros_like(weight)
    return jnp.concatenate(
        [jnp.concatenate([weight, zero], axis=1), jnp.concatenate([zero, weight], axis=1)], axis=0
    )


def halves(wide, nodes, half, hidden):
    return jnp.concatenate(
        [wide[:, :hidden].reshape(nodes, half, hidden), wide[:, hidden:].reshape(nodes, half, hidden)], axis=1
    )


def columns_kernel(fields, columns, rearranged, scratch):
    half = fields.shape[0] // 2
    nodes = fields.shape[2]
    for pair in range(half):
        column = paired(fields, pair).astype(F32).T
        scratch[pl.ds(pair, nodes, stride=half), :] = column
        columns[pair] = column.astype(BF16)
    rearranged[...] = scratch[...].astype(BF16)


def own_kernel(rearranged, encode, send, receive, sent, received):
    nodes, members, hidden = received.shape
    half = members // 2
    both = block_diagonal(encode[...])
    send_half = send[0] * 0.5
    receive_half = receive[0] * 0.5
    sent[nodes] = jnp.full(sent.shape[1:], NOWHERE, F32)
    step_nodes = 32
    size = step_nodes * half
    for index in range(nodes // step_nodes):
        rows = rearranged[index * size : (index + 1) * size, :]
        stream = halves(dot(rows, both), step_nodes, half, hidden)
        rounded = stream.astype(BF16).reshape(step_nodes * 2 * half, hidden)
        shape = (step_nodes, 2 * half, hidden)
        at = slice(index * step_nodes, (index + 1) * step_nodes)
        sent[at] = dot(rounded, send_half).astype(BF16).astype(F32).reshape(shape)
        received[at] = dot(rounded, receive_half).reshape(shape)


def activated(sender, here):
    moved = sender + here
    return moved + moved * jnp.tanh(moved)


def own_message_kernel(halo_total, edges, sent, received, messages, halo_edges):
    nodes, members, hidden = received.shape
    degree = edges.shape[0]
    group = 8

    def step(index, count):
        for offset in range(group):
            node = index * group + offset
            here = received[node]
            total = None
            for slot in range(degree):
                sender = edges[slot, node]
                value = activated(sent[jnp.minimum(sender, nodes)], here)
                total = value if total is None else total + value
                halo_edges[count] = node * halo_total + sender - nodes
                count = count + jnp.where(sender < nodes, 0, 1)
            messages[node] = total
        return count

    count = lax.fori_loop(0, nodes // group, step, 0)
    for index in range(BATCH):
        halo_edges[count + index] = nodes * halo_total
    halo_edges[halo_edges.shape[0] - 1] = count
    messages[nodes] = jnp.zeros((members, hidden), F32)


def message_kernel(
    halo_count,
    halo_edges_far,
    rearranged,
    received,
    started,
    from_before,
    from_after,
    encode,
    send,
    update,
    gain,
    decode,
    *outputs,
):
    *outs, messages, extended, halo_edges, sems = outputs
    (listed,) = start_copies(sems, (halo_edges_far, halo_edges))
    targets, _ = partners("member")
    nodes, members, hidden = received.shape
    half = members // 2
    regions = len(outs)
    channels = decode.shape[0]
    both = block_diagonal(encode[...])
    send_half = send[0] * 0.5
    for side, source in enumerate((from_before, from_after)):
        stream = halves(dot(source[: halo_count * half, :], both), halo_count, half, hidden)
        rounded = stream.astype(BF16).reshape(halo_count * members, hidden)
        extended[side * halo_count : (side + 1) * halo_count] = (
            dot(rounded, send_half).astype(BF16).astype(F32).reshape(halo_count, members, hidden)
        )

    listed.wait()

    def batch(index, carry):
        found = []
        for offset in range(BATCH):
            code = halo_edges[index * BATCH + offset]
            node = code // (2 * halo_count)
            here = received[jnp.minimum(node, nodes - 1)]
            found.append((node, activated(extended[code % (2 * halo_count)], here)))
        for node, value in found:
            messages[node] = messages[node] + value
        return carry

    lax.fori_loop(0, (halo_edges[halo_edges.shape[0] - 1] + BATCH - 1) // BATCH, batch, 0)
    zero = jnp.zeros_like(decode[...])
    decode_even = jnp.concatenate([decode[...], zero], axis=0)
    decode_odd = jnp.concatenate([zero, decode[...]], axis=0)
    gains = gain[...].astype(F32)
    chunk = nodes // regions
    pairs = chunk // 2
    width = 2 * channels
    average = jnp.full((hidden, width), 1.0 / hidden, BF16)
    low = lax.broadcasted_iota(jnp.int32, (nodes // 2, half, width), 2) < channels
    bases = [target * chunk for target in targets]
    fields = jnp.concatenate(
        [rearranged[pl.ds(pl.multiple_of(base * half, chunk * half), chunk * half), :] for base in bases], axis=0
    )
    stream = halves(dot(fields, both), nodes, half, hidden).reshape(nodes * members, hidden)
    message = jnp.concatenate([messages[pl.ds(base, chunk)] for base in bases], axis=0).reshape(nodes * members, hidden)
    mean_square = dot((message * message).astype(BF16), average)
    scale = lax.rsqrt(mean_square + EPSILON)
    scaled = message * jnp.concatenate([scale] * (hidden // width), axis=1) * gains
    stream = stream + dot(scaled.astype(BF16), update[0])
    final = stream.astype(BF16).reshape(nodes // 2, 2, members, hidden)
    rows = nodes // 2 * members
    change = dot_t(final[:, 0].reshape(rows, hidden), decode_even) + dot_t(
        final[:, 1].reshape(rows, hidden), decode_odd
    )
    wide = fields.astype(F32).reshape(nodes // 2, 2, half, width)
    even, odd = wide[:, 0], wide[:, 1]
    first = jnp.where(low, even, pltpu.roll(odd, channels, 2))
    second = jnp.where(low, pltpu.roll(even, channels, 2), odd)
    initial = jnp.concatenate([first, second], axis=1)
    forecast = (initial + change.reshape(initial.shape)).astype(BF16)
    for index, out in enumerate(outs):
        for pair in range(pairs):
            out[:, pair * width : (pair + 1) * width] = forecast[index * pairs + pair]


def weights_kernel(neighbours, own, before, after, up, down, from_before, from_after, out):
    rows, ensemble = own.shape
    first = from_before.shape[0] - rows
    row_count, column_count = lax.axis_size("member"), lax.axis_size("space")
    own_row, own_column = lax.axis_index("member"), lax.axis_index("space")
    targets, origins = partners("member")
    offsets = []
    for index in range(neighbours.shape[1]):
        region = neighbours[0, index]
        near_row = (region // column_count - own_row + 1 + row_count) % row_count - 1
        near_column = (region % column_count - own_column + 2 + column_count) % column_count - 2
        offsets.append((near_row, near_column))
    sources = {(0, -1): (before, 0), (0, 1): (after, 0), (0, -2): (from_before, first), (0, 2): (from_after, first)}
    for row, source in ((-1, up), (1, down)):
        for index in range(3):
            sources[row, index - 1] = (source, index * rows)
    total = own[...].astype(F32)
    for place, (source, start) in sources.items():
        weight = 0.0
        for near_row, near_column in offsets:
            here = jnp.logical_and(near_row == place[0], near_column == place[1])
            weight = weight + jnp.where(here, 1.0 / (1.0 + (place[0] ** 2 + place[1] ** 2) / 2.0), 0.0)
        total = total + weight * source[start : start + rows, :].astype(F32)
    identity = (
        lax.broadcasted_iota(jnp.int32, (ensemble, ensemble), 0)
        == lax.broadcasted_iota(jnp.int32, (ensemble, ensemble), 1)
    ).astype(F32)
    full = functools.partial(jnp.dot, precision=FULL_PRECISION, preferred_element_type=F32)
    system = identity + total[:ensemble] / (ensemble - 1)
    squares = jnp.sum(jnp.sum(system * system, axis=1, keepdims=True), axis=0, keepdims=True)
    scaling = jnp.sqrt(squares)
    iterate = system / scaling
    correction = 1.5 * identity - 0.5 * iterate
    inverse = correction
    for _ in range(ITERS_NS - 1):
        iterate = full(iterate, correction)
        correction = 1.5 * identity - 0.5 * full(inverse, iterate)
        inverse = full(correction, inverse)
    tail = total[ensemble:]
    forcing = jnp.broadcast_to(tail[0:1] + tail[1:2], (8, ensemble))
    mean_weights = full(full(forcing, inverse), inverse)[0:1] / (scaling * (ensemble - 1))
    transform = inverse / jnp.sqrt(scaling) + mean_weights
    rest = (1.0 - jnp.sum(transform, axis=1, keepdims=True)) / ensemble
    members = ensemble // row_count
    to_rows = lax.broadcasted_iota(jnp.int32, (ensemble, ensemble), 0)
    to_columns = lax.broadcasted_iota(jnp.int32, (ensemble, ensemble), 1)
    wanted_rows, wanted_columns = to_rows % members, to_columns % members
    for index in range(row_count):
        target, origin = targets[index] * members, origins[index] * members
        wanted_rows = wanted_rows + jnp.where(to_rows // members == index, target, 0)
        wanted_columns = wanted_columns + jnp.where(to_columns // members == index, origin, 0)
    by_row = (to_columns == wanted_rows).astype(F32).astype(BF16)
    by_column = (to_rows == wanted_columns).astype(F32).astype(BF16)
    for index, part in enumerate(split(transform + rest)):
        moved = dot(dot(by_row, part).astype(BF16), by_column)
        out[:, index * ensemble : (index + 1) * ensemble] = moved.astype(BF16)


def analysis_kernel(weights, *refs):
    count = len(refs) // 2
    pieces, outs = refs[:count], refs[count:]
    members, width = pieces[0].shape
    step_width = 512
    for start in range(0, width, step_width):
        columns = [piece[:, start : start + step_width] for piece in pieces]
        analysed = dot(weights[...], jnp.concatenate(columns * 2, axis=0)).astype(BF16)
        for index, out in enumerate(outs):
            out[:, start : start + step_width] = analysed[index * members : (index + 1) * members]


def output_kernel(*refs):
    *pieces, far, out, held, scratch, sems = refs
    count = len(pieces)
    members, channels, nodes = out.shape
    half = members // 2
    low = lax.broadcasted_iota(jnp.int32, (half, 2 * channels), 1) < channels
    chunk = nodes // count
    for index, piece in enumerate(pieces):
        held[partners("member")[1][index]] = piece[...]
    for region in range(count):
        for pair in range(chunk // 2):
            block = held[region, :, pair * 2 * channels : (pair + 1) * 2 * channels].astype(F32)
            first, second = block[:half], block[half:]
            row = (region * chunk + 2 * pair) * half
            scratch[row : row + half, :] = jnp.where(low, first, pltpu.roll(second, channels, 1))
            scratch[row + half : row + 2 * half, :] = jnp.where(low, pltpu.roll(first, channels, 1), second)
    copies = []
    for pair in range(half):
        block = scratch[pl.ds(pair, nodes, stride=half), :].T.astype(BF16)
        out[pair] = block[:channels]
        out[pair + half] = block[channels:]
        if (pair + 1) % OUTPUT_STEP == 0:
            step = pair // OUTPUT_STEP
            parts = [slice(start, start + OUTPUT_STEP) for start in (pair + 1 - OUTPUT_STEP, pair + 1 - OUTPUT_STEP + half)]
            copies += start_copies(sems.at[step], *((out.at[part], far.at[part]) for part in parts))
    for copy in copies:
        copy.wait()


def ring(value, axis, shift):
    count = lax.axis_size(axis)
    return lax.ppermute(value, axis, [(i, (i + shift) % count) for i in range(count)])


def partners(axis):
    count = lax.axis_size(axis)
    own = lax.axis_index(axis)
    if count & (count - 1) == 0:
        targets = origins = [own ^ step for step in range(count)]
    else:
        targets = [lax.rem(own + step, count) for step in range(count)]
        origins = [lax.rem(own + count - step, count) for step in range(count)]
    return targets, origins


def exchange(pieces, axis):
    count = lax.axis_size(axis)
    paired_up = count & (count - 1) == 0
    return [pieces[0]] + [
        lax.ppermute(piece, axis, [(i, i ^ step if paired_up else (i + step) % count) for i in range(count)])
        for step, piece in enumerate(pieces)
        if step
    ]


def body(
    initial_fields,
    encode_weight,
    send_weight,
    receive_weight,
    update_weight,
    norm_gain,
    decode_weight,
    edge_senders,
    halo_nodes,
    observed_perturbation,
    observed_values,
    region_neighbours,
):
    members, channels, nodes = initial_fields.shape
    hidden = encode_weight.shape[1]
    half = members // 2
    halo_count = halo_nodes.shape[1]
    ensemble = observed_perturbation.shape[1]
    groups = lax.axis_size("member")
    rows = ensemble + TAIL
    struct = jax.ShapeDtypeStruct
    raw = (initial_fields, encode_weight, send_weight, receive_weight)
    own, *near = call(
        gram_kernel,
        (struct((rows, ensemble), BF16),) + tuple(pltpu.VMEM(value.shape, BF16) for value in raw),
        placed_in(pltpu.HBM, observed_perturbation, observed_values, halo_nodes, *raw),
        specs=[HBM] * 7,
        scratch=[
            pltpu.VMEM(observed_perturbation.shape, BF16),
            pltpu.VMEM(observed_values.shape, BF16),
            pltpu.VMEM(halo_nodes.shape, jnp.int32),
            pltpu.SemaphoreType.DMA((7,)),
        ],
        flops=1 << 24,
    )
    before = ring(own, "space", 1)
    after = ring(own, "space", -1)
    fields, *weights = placed_in(pltpu.VMEM, *near)
    columns, rearranged = call(
        columns_kernel,
        (struct((half, nodes, 2 * channels), BF16), struct((nodes * half, 2 * channels), BF16)),
        (fields,),
        scratch=[pltpu.VMEM((nodes * half, 2 * channels), F32)],
        flops=1 << 28,
    )
    sent, received = call(
        own_kernel,
        (pltpu.VMEM((nodes + 1, members, hidden), F32), pltpu.VMEM((nodes, members, hidden), F32)),
        (rearranged, *weights),
        flops=1 << 30,
    )
    size = halo_count * half
    columns, sent, received = lax.optimization_barrier((columns, sent, received))
    to_before, to_after, column = call(
        functools.partial(pick_kernel, halo_count),
        (struct((size + rows, 2 * channels), BF16),) * 2 + (struct((3 * rows, ensemble), BF16),),
        (columns, own, before, after),
        scratch=[pltpu.VMEM((2 * size, 2 * channels), F32)],
        flops=1 << 27,
    )
    from_before = ring(to_after, "space", 1)
    from_after = ring(to_before, "space", -1)
    edges = edge_senders.T
    started, halo_edges = call(
        functools.partial(own_message_kernel, 2 * halo_count),
        (
            pltpu.VMEM((nodes + 1, members, hidden), F32),
            struct((edges.size + BATCH + 1,), jnp.int32),
        ),
        (edges, *placed_in(pltpu.VMEM, sent, received)),
        specs=[SMEM, VMEM, VMEM],
        outs=(VMEM, SMEM),
        flops=1 << 31,
    )
    column, started = lax.optimization_barrier((column, started))
    up = ring(column, "member", 1)
    down = ring(column, "member", -1)
    width = nodes // groups * channels
    piece = struct((members, width), BF16)
    *predicted, _ = call(
        functools.partial(message_kernel, halo_count),
        (piece,) * groups + (struct(started.shape, F32),),
        (
            halo_edges,
            rearranged,
            *placed_in(pltpu.VMEM, received, started),
            from_before,
            from_after,
            encode_weight,
            send_weight,
            update_weight,
            norm_gain,
            decode_weight.T,
        ),
        specs=[ANY] + [VMEM] * 10,
        scratch=[
            pltpu.VMEM((2 * halo_count, members, hidden), F32),
            pltpu.SMEM(halo_edges.shape, jnp.int32),
            pltpu.SemaphoreType.DMA((1,)),
        ],
        flops=1 << 32,
        aliases={3: groups},
    )
    states = exchange(predicted, "member")
    weights = call(
        weights_kernel,
        struct((ensemble, 2 * ensemble), BF16),
        (region_neighbours, own, before, after, up, down, from_before, from_after),
        specs=[SMEM] + [VMEM] * 7,
        flops=1 << 30,
    )
    analysed = call(
        analysis_kernel,
        (piece,) * groups,
        (weights, *states),
        flops=1 << 28,
    )
    returned = exchange(analysed, "member")
    return call(
        output_kernel,
        struct((members, channels, nodes), BF16),
        tuple(returned),
        outs=HBM,
        scratch=[
            pltpu.VMEM((members, channels, nodes), BF16),
            pltpu.VMEM((groups, members, width), BF16),
            pltpu.VMEM((nodes * half, 2 * channels), F32),
            pltpu.SemaphoreType.DMA((half // OUTPUT_STEP, 2)),
        ],
        flops=1 << 20,
    )


def solution(mesh):
    placed = (
        P("member", None, "space"),
        P(),
        P(),
        P(),
        P(),
        P(),
        P(),
        P("space", None),
        P(None, "space"),
        P(("member", "space"), None, None),
        P(("member", "space"), None, None),
        P(("member", "space"), None),
    )
    return jax.shard_map(
        body, mesh=mesh, in_specs=placed, out_specs=P("member", None, "space"), check_vma=False
    )
```

```python
import functools

import jax
import jax.numpy as jnp
from jax import lax
from jax.experimental import pallas as pl
from jax.experimental.pallas import tpu as pltpu
from jax.sharding import PartitionSpec as P

ITERS_NS = 5
EPSILON = 1e-05
F32 = jnp.float32
BF16 = jnp.bfloat16
FULL_PRECISION = lax.Precision.HIGHEST
VMEM = pl.BlockSpec(memory_space=pltpu.VMEM)
SMEM = pl.BlockSpec(memory_space=pltpu.SMEM)
TAIL = 16
NOWHERE = -1048576.0
OUTPUT_STEP = 4
BATCH = 16
HBM = pl.BlockSpec(memory_space=pltpu.HBM)
ANY = pl.BlockSpec(memory_space=pl.ANY)


def dot(left, right):
    return jnp.dot(left, right, preferred_element_type=F32)


def dot_t(left, right):
    return lax.dot_general(left, right, (((1,), (1,)), ((), ())), preferred_element_type=F32)


def split(value):
    high = value.astype(BF16)
    return high, (value - high.astype(F32)).astype(BF16)


def placed_in(space, *values):
    return tuple(pltpu.with_memory_space_constraint(value, space) for value in values)


def call(kernel, shapes, inputs, specs=None, outs=None, scratch=(), flops=0, aliases=None):
    return pl.pallas_call(
        kernel,
        out_shape=shapes,
        in_specs=specs or [VMEM] * len(inputs),
        out_specs=outs or jax.tree.map(lambda _: VMEM, shapes),
        scratch_shapes=list(scratch),
        input_output_aliases=aliases or {},
        compiler_params=pltpu.CompilerParams(vmem_limit_bytes=16 * 1024 * 1024),
        cost_estimate=pl.CostEstimate(flops=flops, bytes_accessed=1 << 20, transcendentals=0),
    )(*inputs)


def start_copies(sems, *ends):
    copies = [
        pltpu.make_async_copy(source, target, sems.at[index]) for index, (source, target) in enumerate(ends)
    ]
    for copy in copies:
        copy.start()
    return copies


def gram_kernel(perturbation, values, halo_nodes, fields, encode, send, receive, out, *refs):
    *near, held, held_values, held_lists, sems = refs
    copies = start_copies(
        sems,
        (perturbation, held),
        (values, held_values),
        (halo_nodes, held_lists),
        *zip((fields, encode, send, receive), near),
    )
    for copy in copies[:3]:
        copy.wait()
    ensemble = held.shape[1]
    members = held[0]
    wide = held_values[0].astype(F32)
    high, low = split(members.astype(F32) * wide[0:1])
    gram = dot_t(high, members) + dot_t(low, members)
    high, low = split(jnp.broadcast_to(wide[0:1] * wide[1:2], (TAIL, wide.shape[1])))
    forcing = dot_t(high, members) + dot_t(low, members)
    high, low = split(forcing)
    lists = held_lists[...].astype(F32)
    lists = jnp.concatenate([lists, jnp.zeros((2, ensemble - lists.shape[1]), F32)], axis=1)
    row = lax.broadcasted_iota(jnp.int32, forcing.shape, 0)
    tail = jnp.where(row == 0, high.astype(F32), low.astype(F32))
    tail = jnp.where(row == 2, lists[0:1], jnp.where(row == 3, lists[1:2], tail))
    out[:ensemble, :] = gram.astype(BF16)
    out[ensemble:, :] = tail.astype(BF16)
    for copy in copies[3:]:
        copy.wait()


def paired(fields, pair):
    half = fields.shape[0] // 2
    return jnp.concatenate([fields[pair], fields[pair + half]], axis=0)


def pick_kernel(halo_count, columns, own, before, after, to_before, to_after, column, scratch):
    half, nodes, _ = columns.shape
    rows = before.shape[0]
    ensemble = rows - TAIL
    wanted_before = before[ensemble:, :].astype(F32)[3:4]
    wanted_after = after[ensemble:, :].astype(F32)[2:3]
    node = lax.broadcasted_iota(jnp.int32, (nodes, wanted_before.shape[1]), 0).astype(F32)
    chosen = jnp.concatenate(
        [(node == wanted).astype(F32).T[:halo_count].astype(BF16) for wanted in (wanted_before, wanted_after)],
        axis=0,
    )
    for pair in range(half):
        picked = dot(chosen, columns[pair])
        scratch[pl.ds(pair, 2 * halo_count, stride=half), :] = picked
    size = halo_count * half
    to_before[:size, :] = scratch[:size, :].astype(BF16)
    to_after[:size, :] = scratch[size:, :].astype(BF16)
    to_before[size:, :] = after[...]
    to_after[size:, :] = before[...]
    for index, source in enumerate((before, own, after)):
        column[index * rows : (index + 1) * rows, :] = source[...]


def block_diagonal(weight):
    zero = jnp.zeros_like(weight)
    return jnp.concatenate(
        [jnp.concatenate([weight, zero], axis=1), jnp.concatenate([zero, weight], axis=1)], axis=0
    )


def halves(wide, nodes, half, hidden):
    return jnp.concatenate(
        [wide[:, :hidden].reshape(nodes, half, hidden), wide[:, hidden:].reshape(nodes, half, hidden)], axis=1
    )


def columns_kernel(fields, columns, rearranged, scratch):
    half = fields.shape[0] // 2
    nodes = fields.shape[2]
    for pair in range(half):
        column = paired(fields, pair).astype(F32).T
        scratch[pl.ds(pair, nodes, stride=half), :] = column
        columns[pair] = column.astype(BF16)
    rearranged[...] = scratch[...].astype(BF16)


def own_kernel(rearranged, encode, send, receive, sent, received):
    nodes, members, hidden = received.shape
    half = members // 2
    both = block_diagonal(encode[...])
    send_half = send[0] * 0.5
    receive_half = receive[0] * 0.5
    sent[nodes] = jnp.full(sent.shape[1:], NOWHERE, F32)
    step_nodes = 32
    size = step_nodes * half
    for index in range(nodes // step_nodes):
        rows = rearranged[index * size : (index + 1) * size, :]
        stream = halves(dot(rows, both), step_nodes, half, hidden)
        rounded = stream.astype(BF16).reshape(step_nodes * 2 * half, hidden)
        shape = (step_nodes, 2 * half, hidden)
        at = slice(index * step_nodes, (index + 1) * step_nodes)
        sent[at] = dot(rounded, send_half).astype(BF16).astype(F32).reshape(shape)
        received[at] = dot(rounded, receive_half).reshape(shape)


def activated(sender, here):
    moved = sender + here
    return moved + moved * jnp.tanh(moved)


def own_message_kernel(halo_total, edges, sent, received, messages, halo_edges):
    nodes, members, hidden = received.shape
    degree = edges.shape[0]
    group = 8

    def step(index, count):
        for offset in range(group):
            node = index * group + offset
            here = received[node]
            total = None
            for slot in range(degree):
                sender = edges[slot, node]
                value = activated(sent[jnp.minimum(sender, nodes)], here)
                total = value if total is None else total + value
                halo_edges[count] = node * halo_total + sender - nodes
                count = count + jnp.where(sender < nodes, 0, 1)
            messages[node] = total
        return count

    count = lax.fori_loop(0, nodes // group, step, 0)
    for index in range(BATCH):
        halo_edges[count + index] = nodes * halo_total
    halo_edges[halo_edges.shape[0] - 1] = count
    messages[nodes] = jnp.zeros((members, hidden), F32)


def message_kernel(
    halo_count,
    halo_edges_far,
    rearranged,
    received,
    started,
    from_before,
    from_after,
    encode,
    send,
    update,
    gain,
    decode,
    *outputs,
):
    *outs, messages, extended, halo_edges, sems = outputs
    (listed,) = start_copies(sems, (halo_edges_far, halo_edges))
    nodes, members, hidden = received.shape
    half = members // 2
    both = block_diagonal(encode[...])
    send_half = send[0] * 0.5
    for side, source in enumerate((from_before, from_after)):
        stream = halves(dot(source[: halo_count * half, :], both), halo_count, half, hidden)
        rounded = stream.astype(BF16).reshape(halo_count * members, hidden)
        extended[side * halo_count : (side + 1) * halo_count] = (
            dot(rounded, send_half).astype(BF16).astype(F32).reshape(halo_count, members, hidden)
        )

    listed.wait()

    def batch(index, carry):
        found = []
        for offset in range(BATCH):
            code = halo_edges[index * BATCH + offset]
            node = code // (2 * halo_count)
            here = received[jnp.minimum(node, nodes - 1)]
            found.append((node, activated(extended[code % (2 * halo_count)], here)))
        for node, value in found:
            messages[node] = messages[node] + value
        return carry

    lax.fori_loop(0, (halo_edges[halo_edges.shape[0] - 1] + BATCH - 1) // BATCH, batch, 0)
    forecast_kernel(range(1, len(outs) + 1), messages, rearranged, encode, update, gain, decode, *outs)


def forecast_kernel(pieces, messages, rearranged, encode, update, gain, decode, *outs):
    members, hidden = messages.shape[1:]
    half = members // 2
    channels = decode.shape[0]
    targets, _ = partners("member")
    chunk = rearranged.shape[0] // half // len(targets)
    nodes = chunk * len(outs)
    both = block_diagonal(encode[...])
    zero = jnp.zeros_like(decode[...])
    decode_even = jnp.concatenate([decode[...], zero], axis=0)
    decode_odd = jnp.concatenate([zero, decode[...]], axis=0)
    gains = gain[...].astype(F32)
    pairs = chunk // 2
    width = 2 * channels
    average = jnp.full((hidden, width), 1.0 / hidden, BF16)
    low = lax.broadcasted_iota(jnp.int32, (nodes // 2, half, width), 2) < channels
    bases = [target * chunk for target in [targets[piece] for piece in pieces]]
    fields = jnp.concatenate(
        [rearranged[pl.ds(pl.multiple_of(base * half, chunk * half), chunk * half), :] for base in bases], axis=0
    )
    stream = halves(dot(fields, both), nodes, half, hidden).reshape(nodes * members, hidden)
    message = jnp.concatenate([messages[pl.ds(base, chunk)] for base in bases], axis=0).reshape(nodes * members, hidden)
    mean_square = dot((message * message).astype(BF16), average)
    scale = lax.rsqrt(mean_square + EPSILON)
    scaled = message * jnp.concatenate([scale] * (hidden // width), axis=1) * gains
    stream = stream + dot(scaled.astype(BF16), update[0])
    final = stream.astype(BF16).reshape(nodes // 2, 2, members, hidden)
    rows = nodes // 2 * members
    change = dot_t(final[:, 0].reshape(rows, hidden), decode_even) + dot_t(
        final[:, 1].reshape(rows, hidden), decode_odd
    )
    wide = fields.astype(F32).reshape(nodes // 2, 2, half, width)
    even, odd = wide[:, 0], wide[:, 1]
    first = jnp.where(low, even, pltpu.roll(odd, channels, 2))
    second = jnp.where(low, pltpu.roll(even, channels, 2), odd)
    initial = jnp.concatenate([first, second], axis=1)
    forecast = (initial + change.reshape(initial.shape)).astype(BF16)
    for index, out in enumerate(outs):
        for pair in range(pairs):
            out[:, pair * width : (pair + 1) * width] = forecast[index * pairs + pair]


def weights_kernel(neighbours, own, before, after, up, down, from_before, from_after, *refs):
    *forecast, out, piece = refs
    forecast_kernel([0], *forecast, piece)
    rows, ensemble = own.shape
    first = from_before.shape[0] - rows
    row_count, column_count = lax.axis_size("member"), lax.axis_size("space")
    own_row, own_column = lax.axis_index("member"), lax.axis_index("space")
    targets, origins = partners("member")
    offsets = []
    for index in range(neighbours.shape[1]):
        region = neighbours[0, index]
        near_row = (region // column_count - own_row + 1 + row_count) % row_count - 1
        near_column = (region % column_count - own_column + 2 + column_count) % column_count - 2
        offsets.append((near_row, near_column))
    sources = {(0, -1): (before, 0), (0, 1): (after, 0), (0, -2): (from_before, first), (0, 2): (from_after, first)}
    for row, source in ((-1, up), (1, down)):
        for index in range(3):
            sources[row, index - 1] = (source, index * rows)
    total = own[...].astype(F32)
    for place, (source, start) in sources.items():
        weight = 0.0
        for near_row, near_column in offsets:
            here = jnp.logical_and(near_row == place[0], near_column == place[1])
            weight = weight + jnp.where(here, 1.0 / (1.0 + (place[0] ** 2 + place[1] ** 2) / 2.0), 0.0)
        total = total + weight * source[start : start + rows, :].astype(F32)
    identity = (
        lax.broadcasted_iota(jnp.int32, (ensemble, ensemble), 0)
        == lax.broadcasted_iota(jnp.int32, (ensemble, ensemble), 1)
    ).astype(F32)
    full = functools.partial(jnp.dot, precision=FULL_PRECISION, preferred_element_type=F32)
    system = identity + total[:ensemble] / (ensemble - 1)
    squares = jnp.sum(jnp.sum(system * system, axis=1, keepdims=True), axis=0, keepdims=True)
    scaling = jnp.sqrt(squares)
    iterate = system / scaling
    correction = 1.5 * identity - 0.5 * iterate
    inverse = correction
    for _ in range(ITERS_NS - 1):
        iterate = full(iterate, correction)
        correction = 1.5 * identity - 0.5 * full(inverse, iterate)
        inverse = full(correction, inverse)
    tail = total[ensemble:]
    forcing = jnp.broadcast_to(tail[0:1] + tail[1:2], (8, ensemble))
    mean_weights = full(full(forcing, inverse), inverse)[0:1] / (scaling * (ensemble - 1))
    transform = inverse / jnp.sqrt(scaling) + mean_weights
    rest = (1.0 - jnp.sum(transform, axis=1, keepdims=True)) / ensemble
    members = ensemble // row_count
    to_rows = lax.broadcasted_iota(jnp.int32, (ensemble, ensemble), 0)
    to_columns = lax.broadcasted_iota(jnp.int32, (ensemble, ensemble), 1)
    wanted_rows, wanted_columns = to_rows % members, to_columns % members
    for index in range(row_count):
        target, origin = targets[index] * members, origins[index] * members
        wanted_rows = wanted_rows + jnp.where(to_rows // members == index, target, 0)
        wanted_columns = wanted_columns + jnp.where(to_columns // members == index, origin, 0)
    by_row = (to_columns == wanted_rows).astype(F32).astype(BF16)
    by_column = (to_rows == wanted_columns).astype(F32).astype(BF16)
    for index, part in enumerate(split(transform + rest)):
        moved = dot(dot(by_row, part).astype(BF16), by_column)
        out[:, index * ensemble : (index + 1) * ensemble] = moved.astype(BF16)


def analysis_kernel(weights, *refs):
    count = len(refs) // 2
    pieces, outs = refs[:count], refs[count:]
    members, width = pieces[0].shape
    step_width = 512
    for start in range(0, width, step_width):
        columns = [piece[:, start : start + step_width] for piece in pieces]
        analysed = dot(weights[...], jnp.concatenate(columns * 2, axis=0)).astype(BF16)
        for index, out in enumerate(outs):
            out[:, start : start + step_width] = analysed[index * members : (index + 1) * members]


def stage(piece, region, staged):
    members, width = piece.shape
    half = members // 2
    lanes = staged.shape[2]
    low = lax.broadcasted_iota(jnp.int32, (half, lanes), 1) < lanes // 2
    for pair in range(width // lanes):
        block = piece[:, pair * lanes : (pair + 1) * lanes].astype(F32)
        first, second = block[:half], block[half:]
        row = 2 * pair * half
        staged[region, row : row + half, :] = jnp.where(low, first, pltpu.roll(second, lanes // 2, 1))
        staged[region, row + half : row + 2 * half, :] = jnp.where(low, pltpu.roll(first, lanes // 2, 1), second)


def stage_kernel(*refs):
    *pieces, staged = refs
    _, origins = partners("member")
    for index, piece in enumerate(pieces):
        stage(piece, origins[index], staged)


def output_kernel(piece, _, far, staged, out, sems):
    _, origins = partners("member")
    stage(piece, origins[len(origins) - 1], staged)
    members, channels, nodes = out.shape
    half = members // 2
    chunk = nodes // len(origins)
    copies = []
    for pair in range(half):
        block = jnp.concatenate(
            [staged[region, pl.ds(pair, chunk, stride=half), :] for region in range(len(origins))], axis=0
        ).T.astype(BF16)
        out[pair] = block[:channels]
        out[pair + half] = block[channels:]
        if (pair + 1) % OUTPUT_STEP == 0:
            start = pair + 1 - OUTPUT_STEP
            parts = [slice(first, first + OUTPUT_STEP) for first in (start, start + half)]
            copies += start_copies(sems.at[pair // OUTPUT_STEP], *((out.at[part], far.at[part]) for part in parts))
    for copy in copies:
        copy.wait()


def ring(value, axis, shift):
    count = lax.axis_size(axis)
    return lax.ppermute(value, axis, [(i, (i + shift) % count) for i in range(count)])


def partners(axis):
    count = lax.axis_size(axis)
    own = lax.axis_index(axis)
    if count & (count - 1) == 0:
        targets = origins = [own ^ step for step in range(count)]
    else:
        targets = [lax.rem(own + step, count) for step in range(count)]
        origins = [lax.rem(own + count - step, count) for step in range(count)]
    return targets, origins


def exchange(pieces, axis):
    count = lax.axis_size(axis)
    paired_up = count & (count - 1) == 0
    return [pieces[0]] + [
        lax.ppermute(piece, axis, [(i, i ^ step if paired_up else (i + step) % count) for i in range(count)])
        for step, piece in enumerate(pieces)
        if step
    ]


def body(
    initial_fields,
    encode_weight,
    send_weight,
    receive_weight,
    update_weight,
    norm_gain,
    decode_weight,
    edge_senders,
    halo_nodes,
    observed_perturbation,
    observed_values,
    region_neighbours,
):
    members, channels, nodes = initial_fields.shape
    hidden = encode_weight.shape[1]
    half = members // 2
    halo_count = halo_nodes.shape[1]
    ensemble = observed_perturbation.shape[1]
    groups = lax.axis_size("member")
    rows = ensemble + TAIL
    struct = jax.ShapeDtypeStruct
    raw = (initial_fields, encode_weight, send_weight, receive_weight)
    own, *near = call(
        gram_kernel,
        (struct((rows, ensemble), BF16),) + tuple(pltpu.VMEM(value.shape, BF16) for value in raw),
        placed_in(pltpu.HBM, observed_perturbation, observed_values, halo_nodes, *raw),
        specs=[HBM] * 7,
        scratch=[
            pltpu.VMEM(observed_perturbation.shape, BF16),
            pltpu.VMEM(observed_values.shape, BF16),
            pltpu.VMEM(halo_nodes.shape, jnp.int32),
            pltpu.SemaphoreType.DMA((7,)),
        ],
        flops=1 << 24,
    )
    before = ring(own, "space", 1)
    fields, *weights = placed_in(pltpu.VMEM, *near)
    columns, rearranged = call(
        columns_kernel,
        (struct((half, nodes, 2 * channels), BF16), struct((nodes * half, 2 * channels), BF16)),
        (fields,),
        scratch=[pltpu.VMEM((nodes * half, 2 * channels), F32)],
        flops=1 << 28,
    )
    own_again, _ = lax.optimization_barrier((own, columns))
    after = ring(own_again, "space", -1)
    sent, received = call(
        own_kernel,
        (pltpu.VMEM((nodes + 1, members, hidden), F32), pltpu.VMEM((nodes, members, hidden), F32)),
        (rearranged, *weights),
        flops=1 << 30,
    )
    size = halo_count * half
    columns, sent, received = lax.optimization_barrier((columns, sent, received))
    to_before, to_after, column = call(
        functools.partial(pick_kernel, halo_count),
        (struct((size + rows, 2 * channels), BF16),) * 2 + (struct((3 * rows, ensemble), BF16),),
        (columns, own, before, after),
        scratch=[pltpu.VMEM((2 * size, 2 * channels), F32)],
        flops=1 << 27,
    )
    from_before = ring(to_after, "space", 1)
    from_after = ring(to_before, "space", -1)
    edges = edge_senders.T
    started, halo_edges = call(
        functools.partial(own_message_kernel, 2 * halo_count),
        (
            pltpu.VMEM((nodes + 1, members, hidden), F32),
            struct((edges.size + BATCH + 1,), jnp.int32),
        ),
        (edges, *placed_in(pltpu.VMEM, sent, received)),
        specs=[SMEM, VMEM, VMEM],
        outs=(VMEM, SMEM),
        flops=1 << 31,
    )
    column, started = lax.optimization_barrier((column, started))
    up = ring(column, "member", 1)
    down = ring(column, "member", -1)
    width = nodes // groups * channels
    piece = struct((members, width), BF16)
    shared = (rearranged, encode_weight, update_weight, norm_gain, decode_weight.T)
    *predicted, messages = call(
        functools.partial(message_kernel, halo_count),
        (piece,) * (groups - 1) + (pltpu.VMEM(started.shape, F32),),
        (
            halo_edges,
            rearranged,
            *placed_in(pltpu.VMEM, received, started),
            from_before,
            from_after,
            encode_weight,
            send_weight,
            update_weight,
            norm_gain,
            decode_weight.T,
        ),
        specs=[ANY] + [VMEM] * 10,
        scratch=[
            pltpu.VMEM((2 * halo_count, members, hidden), F32),
            pltpu.SMEM(halo_edges.shape, jnp.int32),
            pltpu.SemaphoreType.DMA((1,)),
        ],
        flops=1 << 32,
        aliases={3: groups - 1},
    )
    predicted = exchange([None, *predicted], "member")
    weights, kept = call(
        weights_kernel,
        (struct((ensemble, 2 * ensemble), BF16), piece),
        (
            region_neighbours,
            own,
            before,
            after,
            up,
            down,
            from_before,
            from_after,
            *placed_in(pltpu.VMEM, messages),
            *shared,
        ),
        specs=[SMEM] + [VMEM] * (8 + len(shared)),
        flops=1 << 30,
    )
    states = (kept, *predicted[1:])
    analysed = call(
        analysis_kernel,
        (piece,) * groups,
        (weights, *states),
        flops=1 << 28,
    )
    *early_pieces, last_piece = exchange(analysed, "member")
    staged = call(
        stage_kernel,
        pltpu.VMEM((groups, nodes // groups * half, 2 * channels), F32),
        tuple(early_pieces),
        flops=1 << 24,
    )
    analysis, _ = call(
        output_kernel,
        (struct((members, channels, nodes), BF16), pltpu.VMEM(staged.shape, F32)),
        (last_piece, *placed_in(pltpu.VMEM, staged)),
        outs=(HBM, VMEM),
        scratch=[
            pltpu.VMEM((members, channels, nodes), BF16),
            pltpu.SemaphoreType.DMA((half // OUTPUT_STEP, 2)),
        ],
        flops=1 << 24,
        aliases={1: 1},
    )
    return analysis


def solution(mesh):
    placed = (
        P("member", None, "space"),
        P(),
        P(),
        P(),
        P(),
        P(),
        P(),
        P("space", None),
        P(None, "space"),
        P(("member", "space"), None, None),
        P(("member", "space"), None, None),
        P(("member", "space"), None),
    )
    return jax.shard_map(
        body, mesh=mesh, in_specs=placed, out_specs=P("member", None, "space"), check_vma=False
    )
```

```python
import functools

import jax
import jax.numpy as jnp
from jax import lax
from jax.experimental import pallas as pl
from jax.experimental.pallas import tpu as pltpu
from jax.sharding import PartitionSpec as P

ITERS_NS = 5
EPSILON = 1e-05
F32 = jnp.float32
BF16 = jnp.bfloat16
FULL_PRECISION = lax.Precision.HIGHEST
VMEM = pl.BlockSpec(memory_space=pltpu.VMEM)
SMEM = pl.BlockSpec(memory_space=pltpu.SMEM)
TAIL = 16
NOWHERE = -1048576.0
OUTPUT_STEP = 4
BATCH = 16
HBM = pl.BlockSpec(memory_space=pltpu.HBM)
ANY = pl.BlockSpec(memory_space=pl.ANY)


def dot(left, right):
    return jnp.dot(left, right, preferred_element_type=F32)


def dot_t(left, right):
    return lax.dot_general(left, right, (((1,), (1,)), ((), ())), preferred_element_type=F32)


def split(value):
    high = value.astype(BF16)
    return high, (value - high.astype(F32)).astype(BF16)


def placed_in(space, *values):
    return tuple(pltpu.with_memory_space_constraint(value, space) for value in values)


def call(kernel, shapes, inputs, specs=None, outs=None, scratch=(), flops=0, aliases=None):
    return pl.pallas_call(
        kernel,
        out_shape=shapes,
        in_specs=specs or [VMEM] * len(inputs),
        out_specs=outs or jax.tree.map(lambda _: VMEM, shapes),
        scratch_shapes=list(scratch),
        input_output_aliases=aliases or {},
        compiler_params=pltpu.CompilerParams(vmem_limit_bytes=16 * 1024 * 1024),
        cost_estimate=pl.CostEstimate(flops=flops, bytes_accessed=1 << 20, transcendentals=0),
    )(*inputs)


def start_copies(sems, *ends):
    copies = [
        pltpu.make_async_copy(source, target, sems.at[index]) for index, (source, target) in enumerate(ends)
    ]
    for copy in copies:
        copy.start()
    return copies


def gram_kernel(perturbation, values, halo_nodes, fields, encode, send, receive, out, *refs):
    *near, held, held_values, held_lists, sems = refs
    copies = start_copies(
        sems,
        (perturbation, held),
        (values, held_values),
        (halo_nodes, held_lists),
        *zip((fields, encode, send, receive), near),
    )
    for copy in copies[:3]:
        copy.wait()
    ensemble = held.shape[1]
    members = held[0]
    wide = held_values[0].astype(F32)
    high, low = split(members.astype(F32) * wide[0:1])
    gram = dot_t(high, members) + dot_t(low, members)
    high, low = split(jnp.broadcast_to(wide[0:1] * wide[1:2], (TAIL, wide.shape[1])))
    forcing = dot_t(high, members) + dot_t(low, members)
    high, low = split(forcing)
    lists = held_lists[...].astype(F32)
    lists = jnp.concatenate([lists, jnp.zeros((2, ensemble - lists.shape[1]), F32)], axis=1)
    row = lax.broadcasted_iota(jnp.int32, forcing.shape, 0)
    tail = jnp.where(row == 0, high.astype(F32), low.astype(F32))
    tail = jnp.where(row == 2, lists[0:1], jnp.where(row == 3, lists[1:2], tail))
    out[:ensemble, :] = gram.astype(BF16)
    out[ensemble:, :] = tail.astype(BF16)
    for copy in copies[3:]:
        copy.wait()


def paired(fields, pair):
    half = fields.shape[0] // 2
    return jnp.concatenate([fields[pair], fields[pair + half]], axis=0)


def pick_kernel(halo_count, columns, own, before, after, to_before, to_after, column, scratch):
    half, nodes, _ = columns.shape
    rows = before.shape[0]
    ensemble = rows - TAIL
    wanted_before = before[ensemble:, :].astype(F32)[3:4]
    wanted_after = after[ensemble:, :].astype(F32)[2:3]
    node = lax.broadcasted_iota(jnp.int32, (nodes, wanted_before.shape[1]), 0).astype(F32)
    chosen = jnp.concatenate(
        [(node == wanted).astype(F32).T[:halo_count].astype(BF16) for wanted in (wanted_before, wanted_after)],
        axis=0,
    )
    for pair in range(half):
        picked = dot(chosen, columns[pair])
        scratch[pl.ds(pair, 2 * halo_count, stride=half), :] = picked
    size = halo_count * half
    to_before[:size, :] = scratch[:size, :].astype(BF16)
    to_after[:size, :] = scratch[size:, :].astype(BF16)
    to_before[size:, :] = after[...]
    to_after[size:, :] = before[...]
    for index, source in enumerate((before, own, after)):
        column[index * rows : (index + 1) * rows, :] = source[...]


def block_diagonal(weight):
    zero = jnp.zeros_like(weight)
    return jnp.concatenate(
        [jnp.concatenate([weight, zero], axis=1), jnp.concatenate([zero, weight], axis=1)], axis=0
    )


def halves(wide, nodes, half, hidden):
    return jnp.concatenate(
        [wide[:, :hidden].reshape(nodes, half, hidden), wide[:, hidden:].reshape(nodes, half, hidden)], axis=1
    )


def columns_kernel(fields, columns, rearranged, scratch):
    half = fields.shape[0] // 2
    nodes = fields.shape[2]
    for pair in range(half):
        column = paired(fields, pair).astype(F32).T
        scratch[pl.ds(pair, nodes, stride=half), :] = column
        columns[pair] = column.astype(BF16)
    rearranged[...] = scratch[...].astype(BF16)


def own_kernel(rearranged, encode, send, receive, sent, received):
    nodes, members, hidden = received.shape
    half = members // 2
    both = block_diagonal(encode[...])
    send_half = send[0] * 0.5
    receive_half = receive[0] * 0.5
    sent[nodes] = jnp.full(sent.shape[1:], NOWHERE, F32)
    step_nodes = 32
    size = step_nodes * half
    for index in range(nodes // step_nodes):
        rows = rearranged[index * size : (index + 1) * size, :]
        stream = halves(dot(rows, both), step_nodes, half, hidden)
        rounded = stream.astype(BF16).reshape(step_nodes * 2 * half, hidden)
        shape = (step_nodes, 2 * half, hidden)
        at = slice(index * step_nodes, (index + 1) * step_nodes)
        sent[at] = dot(rounded, send_half).astype(BF16).astype(F32).reshape(shape)
        received[at] = dot(rounded, receive_half).reshape(shape)


def activated(sender, here):
    moved = sender + here
    return moved + moved * jnp.tanh(moved)


def own_message_kernel(halo_total, edges, sent, received, messages, halo_edges):
    nodes, members, hidden = received.shape
    degree = edges.shape[0]
    group = 8

    def step(index, count):
        for offset in range(group):
            node = index * group + offset
            here = received[node]
            total = None
            for slot in range(degree):
                sender = edges[slot, node]
                value = activated(sent[jnp.minimum(sender, nodes)], here)
                total = value if total is None else total + value
                halo_edges[count] = node * halo_total + sender - nodes
                count = count + jnp.where(sender < nodes, 0, 1)
            messages[node] = total
        return count

    count = lax.fori_loop(0, nodes // group, step, 0)
    for index in range(BATCH):
        halo_edges[count + index] = nodes * halo_total
    halo_edges[halo_edges.shape[0] - 1] = count
    messages[nodes] = jnp.zeros((members, hidden), F32)


def message_kernel(
    halo_count,
    halo_edges_far,
    rearranged,
    received,
    started,
    from_before,
    from_after,
    encode,
    send,
    update,
    gain,
    decode,
    *outputs,
):
    *outs, messages, extended, halo_edges, sems = outputs
    (listed,) = start_copies(sems, (halo_edges_far, halo_edges))
    nodes, members, hidden = received.shape
    half = members // 2
    both = block_diagonal(encode[...])
    send_half = send[0] * 0.5
    for side, source in enumerate((from_before, from_after)):
        stream = halves(dot(source[: halo_count * half, :], both), halo_count, half, hidden)
        rounded = stream.astype(BF16).reshape(halo_count * members, hidden)
        extended[side * halo_count : (side + 1) * halo_count] = (
            dot(rounded, send_half).astype(BF16).astype(F32).reshape(halo_count, members, hidden)
        )

    listed.wait()

    def batch(index, carry):
        found = []
        for offset in range(BATCH):
            code = halo_edges[index * BATCH + offset]
            node = code // (2 * halo_count)
            here = received[jnp.minimum(node, nodes - 1)]
            found.append((node, activated(extended[code % (2 * halo_count)], here)))
        for node, value in found:
            messages[node] = messages[node] + value
        return carry

    lax.fori_loop(0, (halo_edges[halo_edges.shape[0] - 1] + BATCH - 1) // BATCH, batch, 0)
    forecast_kernel(range(1, len(outs) + 1), messages, rearranged, encode, update, gain, decode, *outs)


def forecast_kernel(pieces, messages, rearranged, encode, update, gain, decode, *outs):
    members, hidden = messages.shape[1:]
    half = members // 2
    channels = decode.shape[0]
    targets, _ = partners("member")
    chunk = rearranged.shape[0] // half // len(targets)
    nodes = chunk * len(outs)
    both = block_diagonal(encode[...])
    zero = jnp.zeros_like(decode[...])
    decode_even = jnp.concatenate([decode[...], zero], axis=0)
    decode_odd = jnp.concatenate([zero, decode[...]], axis=0)
    gains = gain[...].astype(F32)
    pairs = chunk // 2
    width = 2 * channels
    average = jnp.full((hidden, width), 1.0 / hidden, BF16)
    low = lax.broadcasted_iota(jnp.int32, (nodes // 2, half, width), 2) < channels
    bases = [target * chunk for target in [targets[piece] for piece in pieces]]
    fields = jnp.concatenate(
        [rearranged[pl.ds(pl.multiple_of(base * half, chunk * half), chunk * half), :] for base in bases], axis=0
    )
    stream = halves(dot(fields, both), nodes, half, hidden).reshape(nodes * members, hidden)
    message = jnp.concatenate([messages[pl.ds(base, chunk)] for base in bases], axis=0).reshape(nodes * members, hidden)
    mean_square = dot((message * message).astype(BF16), average)
    scale = lax.rsqrt(mean_square + EPSILON)
    scaled = message * jnp.concatenate([scale] * (hidden // width), axis=1) * gains
    stream = stream + dot(scaled.astype(BF16), update[0])
    final = stream.astype(BF16).reshape(nodes // 2, 2, members, hidden)
    rows = nodes // 2 * members
    change = dot_t(final[:, 0].reshape(rows, hidden), decode_even) + dot_t(
        final[:, 1].reshape(rows, hidden), decode_odd
    )
    wide = fields.astype(F32).reshape(nodes // 2, 2, half, width)
    even, odd = wide[:, 0], wide[:, 1]
    first = jnp.where(low, even, pltpu.roll(odd, channels, 2))
    second = jnp.where(low, pltpu.roll(even, channels, 2), odd)
    initial = jnp.concatenate([first, second], axis=1)
    forecast = (initial + change.reshape(initial.shape)).astype(BF16)
    for index, out in enumerate(outs):
        for pair in range(pairs):
            out[:, pair * width : (pair + 1) * width] = forecast[index * pairs + pair]


def weights_kernel(neighbours, own, before, after, down, up, from_before, from_after, *refs):
    *forecast, out, piece = refs
    forecast_kernel([0], *forecast, piece)
    rows, ensemble = own.shape
    first = from_before.shape[0] - rows
    row_count, column_count = lax.axis_size("member"), lax.axis_size("space")
    own_row, own_column = lax.axis_index("member"), lax.axis_index("space")
    targets, origins = partners("member")
    offsets = []
    for index in range(neighbours.shape[1]):
        region = neighbours[0, index]
        near_row = (region // column_count - own_row + 1 + row_count) % row_count - 1
        near_column = (region % column_count - own_column + 2 + column_count) % column_count - 2
        offsets.append((near_row, near_column))
    sources = {(0, -1): (before, 0), (0, 1): (after, 0), (0, -2): (from_before, first), (0, 2): (from_after, first)}
    for row, source in ((-1, up), (1, down)):
        for index in range(3):
            sources[row, index - 1] = (source, index * rows)
    total = own[...].astype(F32)
    for place, (source, start) in sources.items():
        weight = 0.0
        for near_row, near_column in offsets:
            here = jnp.logical_and(near_row == place[0], near_column == place[1])
            weight = weight + jnp.where(here, 1.0 / (1.0 + (place[0] ** 2 + place[1] ** 2) / 2.0), 0.0)
        total = total + weight * source[start : start + rows, :].astype(F32)
    identity = (
        lax.broadcasted_iota(jnp.int32, (ensemble, ensemble), 0)
        == lax.broadcasted_iota(jnp.int32, (ensemble, ensemble), 1)
    ).astype(F32)
    full = functools.partial(jnp.dot, precision=FULL_PRECISION, preferred_element_type=F32)
    system = identity + total[:ensemble] / (ensemble - 1)
    squares = jnp.sum(jnp.sum(system * system, axis=1, keepdims=True), axis=0, keepdims=True)
    scaling = jnp.sqrt(squares)
    iterate = system / scaling
    correction = 1.5 * identity - 0.5 * iterate
    inverse = correction
    for _ in range(ITERS_NS - 1):
        iterate = full(iterate, correction)
        correction = 1.5 * identity - 0.5 * full(inverse, iterate)
        inverse = full(correction, inverse)
    tail = total[ensemble:]
    forcing = jnp.broadcast_to(tail[0:1] + tail[1:2], (8, ensemble))
    mean_weights = full(full(forcing, inverse), inverse)[0:1] / (scaling * (ensemble - 1))
    transform = inverse / jnp.sqrt(scaling) + mean_weights
    rest = (1.0 - jnp.sum(transform, axis=1, keepdims=True)) / ensemble
    members = ensemble // row_count
    to_rows = lax.broadcasted_iota(jnp.int32, (ensemble, ensemble), 0)
    to_columns = lax.broadcasted_iota(jnp.int32, (ensemble, ensemble), 1)
    wanted_rows, wanted_columns = to_rows % members, to_columns % members
    for index in range(row_count):
        target, origin = targets[index] * members, origins[index] * members
        wanted_rows = wanted_rows + jnp.where(to_rows // members == index, target, 0)
        wanted_columns = wanted_columns + jnp.where(to_columns // members == index, origin, 0)
    by_row = (to_columns == wanted_rows).astype(F32).astype(BF16)
    by_column = (to_rows == wanted_columns).astype(F32).astype(BF16)
    for index, part in enumerate(split(transform + rest)):
        moved = dot(dot(by_row, part).astype(BF16), by_column)
        out[:, index * ensemble : (index + 1) * ensemble] = moved.astype(BF16)


def analysis_kernel(weights, *refs):
    count = len(refs) // 2
    pieces, outs = refs[:count][::-1], refs[count:]
    members, width = pieces[0].shape
    step_width = 512
    for start in range(0, width, step_width):
        columns = [piece[:, start : start + step_width] for piece in pieces]
        analysed = dot(weights[...], jnp.concatenate(columns * 2, axis=0)).astype(BF16)
        for index, out in enumerate(outs):
            out[:, start : start + step_width] = analysed[index * members : (index + 1) * members]


def stage(piece, region, staged):
    members, width = piece.shape
    half = members // 2
    lanes = staged.shape[2]
    low = lax.broadcasted_iota(jnp.int32, (half, lanes), 1) < lanes // 2
    for pair in range(width // lanes):
        block = piece[:, pair * lanes : (pair + 1) * lanes].astype(F32)
        first, second = block[:half], block[half:]
        row = 2 * pair * half
        staged[region, row : row + half, :] = jnp.where(low, first, pltpu.roll(second, lanes // 2, 1))
        staged[region, row + half : row + 2 * half, :] = jnp.where(low, pltpu.roll(first, lanes // 2, 1), second)


def stage_kernel(order, *refs):
    *pieces, staged = refs
    _, origins = partners("member")
    for index, piece in zip(order, pieces):
        stage(piece, origins[index], staged)


def output_kernel(last, piece, _, far, staged, out, sems):
    _, origins = partners("member")
    stage(piece, origins[last], staged)
    members, channels, nodes = out.shape
    half = members // 2
    chunk = nodes // len(origins)
    copies = []
    for pair in range(half):
        block = jnp.concatenate(
            [staged[region, pl.ds(pair, chunk, stride=half), :] for region in range(len(origins))], axis=0
        ).T.astype(BF16)
        out[pair] = block[:channels]
        out[pair + half] = block[channels:]
        if (pair + 1) % OUTPUT_STEP == 0:
            start = pair + 1 - OUTPUT_STEP
            parts = [slice(first, first + OUTPUT_STEP) for first in (start, start + half)]
            copies += start_copies(sems.at[pair // OUTPUT_STEP], *((out.at[part], far.at[part]) for part in parts))
    for copy in copies:
        copy.wait()


def ring(value, axis, shift):
    count = lax.axis_size(axis)
    return lax.ppermute(value, axis, [(i, (i + shift) % count) for i in range(count)])


def partners(axis):
    count = lax.axis_size(axis)
    own = lax.axis_index(axis)
    if count & (count - 1) == 0:
        targets = origins = [own ^ step for step in range(count)]
    else:
        targets = [lax.rem(own + step, count) for step in range(count)]
        origins = [lax.rem(own + count - step, count) for step in range(count)]
    return targets, origins


def exchange(pieces, axis):
    count = lax.axis_size(axis)
    paired_up = count & (count - 1) == 0
    return [pieces[0]] + [
        lax.ppermute(piece, axis, [(i, i ^ step if paired_up else (i + step) % count) for i in range(count)])
        for step, piece in enumerate(pieces)
        if step
    ]


def body(
    initial_fields,
    encode_weight,
    send_weight,
    receive_weight,
    update_weight,
    norm_gain,
    decode_weight,
    edge_senders,
    halo_nodes,
    observed_perturbation,
    observed_values,
    region_neighbours,
):
    members, channels, nodes = initial_fields.shape
    hidden = encode_weight.shape[1]
    half = members // 2
    halo_count = halo_nodes.shape[1]
    ensemble = observed_perturbation.shape[1]
    groups = lax.axis_size("member")
    rows = ensemble + TAIL
    struct = jax.ShapeDtypeStruct
    raw = (initial_fields, encode_weight, send_weight, receive_weight)
    own, *near = call(
        gram_kernel,
        (struct((rows, ensemble), BF16),) + tuple(pltpu.VMEM(value.shape, BF16) for value in raw),
        placed_in(pltpu.HBM, observed_perturbation, observed_values, halo_nodes, *raw),
        specs=[HBM] * 7,
        scratch=[
            pltpu.VMEM(observed_perturbation.shape, BF16),
            pltpu.VMEM(observed_values.shape, BF16),
            pltpu.VMEM(halo_nodes.shape, jnp.int32),
            pltpu.SemaphoreType.DMA((7,)),
        ],
        flops=1 << 24,
    )
    before = ring(own, "space", 1)
    fields, *weights = placed_in(pltpu.VMEM, *near)
    columns, rearranged = call(
        columns_kernel,
        (struct((half, nodes, 2 * channels), BF16), struct((nodes * half, 2 * channels), BF16)),
        (fields,),
        scratch=[pltpu.VMEM((nodes * half, 2 * channels), F32)],
        flops=1 << 28,
    )
    own_again, _ = lax.optimization_barrier((own, columns))
    after = ring(own_again, "space", -1)
    sent, received = call(
        own_kernel,
        (pltpu.VMEM((nodes + 1, members, hidden), F32), pltpu.VMEM((nodes, members, hidden), F32)),
        (rearranged, *weights),
        flops=1 << 30,
    )
    size = halo_count * half
    columns, sent, received = lax.optimization_barrier((columns, sent, received))
    to_before, to_after, column = call(
        functools.partial(pick_kernel, halo_count),
        (struct((size + rows, 2 * channels), BF16),) * 2 + (struct((3 * rows, ensemble), BF16),),
        (columns, own, before, after),
        scratch=[pltpu.VMEM((2 * size, 2 * channels), F32)],
        flops=1 << 27,
    )
    from_before = ring(to_after, "space", 1)
    from_after = ring(to_before, "space", -1)
    edges = edge_senders.T
    started, halo_edges = call(
        functools.partial(own_message_kernel, 2 * halo_count),
        (
            pltpu.VMEM((nodes + 1, members, hidden), F32),
            struct((edges.size + BATCH + 1,), jnp.int32),
        ),
        (edges, *placed_in(pltpu.VMEM, sent, received)),
        specs=[SMEM, VMEM, VMEM],
        outs=(VMEM, SMEM),
        flops=1 << 31,
    )
    column, started = lax.optimization_barrier((column, started))
    down = ring(column, "member", -1)
    up = ring(column, "member", 1)
    width = nodes // groups * channels
    piece = struct((members, width), BF16)
    shared = (rearranged, encode_weight, update_weight, norm_gain, decode_weight.T)
    *predicted, messages = call(
        functools.partial(message_kernel, halo_count),
        (piece,) * (groups - 1) + (pltpu.VMEM(started.shape, F32),),
        (
            halo_edges,
            rearranged,
            *placed_in(pltpu.VMEM, received, started),
            from_before,
            from_after,
            encode_weight,
            send_weight,
            update_weight,
            norm_gain,
            decode_weight.T,
        ),
        specs=[ANY] + [VMEM] * 10,
        scratch=[
            pltpu.VMEM((2 * halo_count, members, hidden), F32),
            pltpu.SMEM(halo_edges.shape, jnp.int32),
            pltpu.SemaphoreType.DMA((1,)),
        ],
        flops=1 << 32,
        aliases={3: groups - 1},
    )
    predicted = exchange([None, *predicted], "member")
    weights, kept = call(
        weights_kernel,
        (struct((ensemble, 2 * ensemble), BF16), piece),
        (
            region_neighbours,
            own,
            before,
            after,
            down,
            up,
            from_before,
            from_after,
            *placed_in(pltpu.VMEM, messages),
            *shared,
        ),
        specs=[SMEM] + [VMEM] * (8 + len(shared)),
        flops=1 << 30,
    )
    states = (kept, *predicted[1:])
    analysed = call(
        analysis_kernel,
        (piece,) * groups,
        (weights, *states[::-1]),
        flops=1 << 28,
    )
    returned = exchange(analysed, "member")
    *order, last = [*range(1, groups)][::-1]
    order = [*order, 0]
    staged = call(
        functools.partial(stage_kernel, order),
        pltpu.VMEM((groups, nodes // groups * half, 2 * channels), F32),
        tuple(returned[index] for index in order),
        flops=1 << 24,
    )
    analysis, _ = call(
        functools.partial(output_kernel, last),
        (struct((members, channels, nodes), BF16), pltpu.VMEM(staged.shape, F32)),
        (returned[last], *placed_in(pltpu.VMEM, staged)),
        outs=(HBM, VMEM),
        scratch=[
            pltpu.VMEM((members, channels, nodes), BF16),
            pltpu.SemaphoreType.DMA((half // OUTPUT_STEP, 2)),
        ],
        flops=1 << 24,
        aliases={1: 1},
    )
    return analysis


def solution(mesh):
    placed = (
        P("member", None, "space"),
        P(),
        P(),
        P(),
        P(),
        P(),
        P(),
        P("space", None),
        P(None, "space"),
        P(("member", "space"), None, None),
        P(("member", "space"), None, None),
        P(("member", "space"), None),
    )
    return jax.shard_map(
        body, mesh=mesh, in_specs=placed, out_specs=P("member", None, "space"), check_vma=False
    )
```

```python
import functools

import jax
import jax.numpy as jnp
from jax import lax
from jax.experimental import pallas as pl
from jax.experimental.pallas import tpu as pltpu
from jax.sharding import PartitionSpec as P

ITERS_NS = 5
EPSILON = 1e-05
F32 = jnp.float32
BF16 = jnp.bfloat16
FULL_PRECISION = lax.Precision.HIGHEST
VMEM = pl.BlockSpec(memory_space=pltpu.VMEM)
SMEM = pl.BlockSpec(memory_space=pltpu.SMEM)
TAIL = 16
NOWHERE = -1048576.0
OUTPUT_STEP = 4
BATCH = 16
HBM = pl.BlockSpec(memory_space=pltpu.HBM)
ANY = pl.BlockSpec(memory_space=pl.ANY)


def dot(left, right):
    return jnp.dot(left, right, preferred_element_type=F32)


def dot_t(left, right):
    return lax.dot_general(left, right, (((1,), (1,)), ((), ())), preferred_element_type=F32)


def split(value):
    high = value.astype(BF16)
    return high, (value - high.astype(F32)).astype(BF16)


def placed_in(space, *values):
    return tuple(pltpu.with_memory_space_constraint(value, space) for value in values)


def call(kernel, shapes, inputs, specs=None, outs=None, scratch=(), flops=0, aliases=None):
    return pl.pallas_call(
        kernel,
        out_shape=shapes,
        in_specs=specs or [VMEM] * len(inputs),
        out_specs=outs or jax.tree.map(lambda _: VMEM, shapes),
        scratch_shapes=list(scratch),
        input_output_aliases=aliases or {},
        compiler_params=pltpu.CompilerParams(vmem_limit_bytes=16 * 1024 * 1024),
        cost_estimate=pl.CostEstimate(flops=flops, bytes_accessed=1 << 20, transcendentals=0),
    )(*inputs)


def start_copies(sems, *ends):
    copies = [
        pltpu.make_async_copy(source, target, sems.at[index]) for index, (source, target) in enumerate(ends)
    ]
    for copy in copies:
        copy.start()
    return copies


def gram_kernel(perturbation, values, halo_nodes, fields, encode, send, receive, out, *refs):
    *near, held, held_values, held_lists, sems = refs
    copies = start_copies(
        sems,
        (perturbation, held),
        (values, held_values),
        (halo_nodes, held_lists),
        *zip((fields, encode, send, receive), near),
    )
    for copy in copies[:3]:
        copy.wait()
    ensemble = held.shape[1]
    members = held[0]
    wide = held_values[0].astype(F32)
    high, low = split(members.astype(F32) * wide[0:1])
    gram = dot_t(high, members) + dot_t(low, members)
    high, low = split(jnp.broadcast_to(wide[0:1] * wide[1:2], (TAIL, wide.shape[1])))
    forcing = dot_t(high, members) + dot_t(low, members)
    high, low = split(forcing)
    lists = held_lists[...].astype(F32)
    lists = jnp.concatenate([lists, jnp.zeros((2, ensemble - lists.shape[1]), F32)], axis=1)
    row = lax.broadcasted_iota(jnp.int32, forcing.shape, 0)
    tail = jnp.where(row == 0, high.astype(F32), low.astype(F32))
    tail = jnp.where(row == 2, lists[0:1], jnp.where(row == 3, lists[1:2], tail))
    out[:ensemble, :] = gram.astype(BF16)
    out[ensemble:, :] = tail.astype(BF16)
    for copy in copies[3:]:
        copy.wait()


def paired(fields, pair):
    half = fields.shape[0] // 2
    return jnp.concatenate([fields[pair], fields[pair + half]], axis=0)


def pick_kernel(halo_count, columns, own, before, after, to_before, to_after, column, scratch):
    half, nodes, _ = columns.shape
    rows = before.shape[0]
    ensemble = rows - TAIL
    wanted_before = before[ensemble:, :].astype(F32)[3:4]
    wanted_after = after[ensemble:, :].astype(F32)[2:3]
    node = lax.broadcasted_iota(jnp.int32, (nodes, wanted_before.shape[1]), 0).astype(F32)
    chosen = jnp.concatenate(
        [(node == wanted).astype(F32).T[:halo_count].astype(BF16) for wanted in (wanted_before, wanted_after)],
        axis=0,
    )
    for pair in range(half):
        picked = dot(chosen, columns[pair])
        scratch[pl.ds(pair, 2 * halo_count, stride=half), :] = picked
    size = halo_count * half
    to_before[:size, :] = scratch[:size, :].astype(BF16)
    to_after[:size, :] = scratch[size:, :].astype(BF16)
    to_before[size:, :] = after[...]
    to_after[size:, :] = before[...]
    for index, source in enumerate((before, own, after)):
        column[index * rows : (index + 1) * rows, :] = source[...]


def block_diagonal(weight):
    zero = jnp.zeros_like(weight)
    return jnp.concatenate(
        [jnp.concatenate([weight, zero], axis=1), jnp.concatenate([zero, weight], axis=1)], axis=0
    )


def halves(wide, nodes, half, hidden):
    return jnp.concatenate(
        [wide[:, :hidden].reshape(nodes, half, hidden), wide[:, hidden:].reshape(nodes, half, hidden)], axis=1
    )


def columns_kernel(fields, columns, rearranged, scratch):
    half = fields.shape[0] // 2
    nodes = fields.shape[2]
    for pair in range(half):
        column = paired(fields, pair).astype(F32).T
        scratch[pl.ds(pair, nodes, stride=half), :] = column
        columns[pair] = column.astype(BF16)
    rearranged[...] = scratch[...].astype(BF16)


def own_kernel(rearranged, encode, send, receive, sent, received):
    nodes, members, hidden = received.shape
    half = members // 2
    both = block_diagonal(encode[...])
    send_half = send[0] * 0.5
    receive_half = receive[0] * 0.5
    sent[nodes] = jnp.full(sent.shape[1:], NOWHERE, F32)
    step_nodes = 32
    size = step_nodes * half
    for index in range(nodes // step_nodes):
        rows = rearranged[index * size : (index + 1) * size, :]
        stream = halves(dot(rows, both), step_nodes, half, hidden)
        rounded = stream.astype(BF16).reshape(step_nodes * 2 * half, hidden)
        shape = (step_nodes, 2 * half, hidden)
        at = slice(index * step_nodes, (index + 1) * step_nodes)
        sent[at] = dot(rounded, send_half).astype(BF16).astype(F32).reshape(shape)
        received[at] = dot(rounded, receive_half).reshape(shape)


def activated(sender, here):
    moved = sender + here
    return moved + moved * jnp.tanh(moved)


def own_message_kernel(halo_total, edges, sent, received, messages, halo_edges):
    nodes, members, hidden = received.shape
    degree = edges.shape[0]
    group = 8

    def step(index, count):
        for offset in range(group):
            node = index * group + offset
            here = received[node]
            total = None
            for slot in range(degree):
                sender = edges[slot, node]
                value = activated(sent[jnp.minimum(sender, nodes)], here)
                total = value if total is None else total + value
                halo_edges[count] = node * halo_total + sender - nodes
                count = count + jnp.where(sender < nodes, 0, 1)
            messages[node] = total
        return count

    count = lax.fori_loop(0, nodes // group, step, 0)
    for index in range(BATCH):
        halo_edges[count + index] = nodes * halo_total
    halo_edges[halo_edges.shape[0] - 1] = count
    messages[nodes] = jnp.zeros((members, hidden), F32)


def message_kernel(
    halo_count,
    halo_edges_far,
    rearranged,
    received,
    started,
    from_after,
    from_before,
    encode,
    send,
    update,
    gain,
    decode,
    *outputs,
):
    *outs, messages, extended, halo_edges, sems = outputs
    (listed,) = start_copies(sems, (halo_edges_far, halo_edges))
    nodes, members, hidden = received.shape
    half = members // 2
    both = block_diagonal(encode[...])
    send_half = send[0] * 0.5
    for side, source in enumerate((from_before, from_after)):
        stream = halves(dot(source[: halo_count * half, :], both), halo_count, half, hidden)
        rounded = stream.astype(BF16).reshape(halo_count * members, hidden)
        extended[side * halo_count : (side + 1) * halo_count] = (
            dot(rounded, send_half).astype(BF16).astype(F32).reshape(halo_count, members, hidden)
        )

    listed.wait()

    def batch(index, carry):
        found = []
        for offset in range(BATCH):
            code = halo_edges[index * BATCH + offset]
            node = code // (2 * halo_count)
            here = received[jnp.minimum(node, nodes - 1)]
            found.append((node, activated(extended[code % (2 * halo_count)], here)))
        for node, value in found:
            messages[node] = messages[node] + value
        return carry

    lax.fori_loop(0, (halo_edges[halo_edges.shape[0] - 1] + BATCH - 1) // BATCH, batch, 0)
    forecast_kernel(range(1, len(outs) + 1), messages, rearranged, encode, update, gain, decode, *outs)


def forecast_kernel(pieces, messages, rearranged, encode, update, gain, decode, *outs):
    members, hidden = messages.shape[1:]
    half = members // 2
    channels = decode.shape[0]
    targets, _ = partners("member")
    chunk = rearranged.shape[0] // half // len(targets)
    nodes = chunk * len(outs)
    both = block_diagonal(encode[...])
    zero = jnp.zeros_like(decode[...])
    decode_even = jnp.concatenate([decode[...], zero], axis=0)
    decode_odd = jnp.concatenate([zero, decode[...]], axis=0)
    gains = gain[...].astype(F32)
    pairs = chunk // 2
    width = 2 * channels
    average = jnp.full((hidden, width), 1.0 / hidden, BF16)
    low = lax.broadcasted_iota(jnp.int32, (nodes // 2, half, width), 2) < channels
    bases = [target * chunk for target in [targets[piece] for piece in pieces]]
    fields = jnp.concatenate(
        [rearranged[pl.ds(pl.multiple_of(base * half, chunk * half), chunk * half), :] for base in bases], axis=0
    )
    stream = halves(dot(fields, both), nodes, half, hidden).reshape(nodes * members, hidden)
    message = jnp.concatenate([messages[pl.ds(base, chunk)] for base in bases], axis=0).reshape(nodes * members, hidden)
    mean_square = dot((message * message).astype(BF16), average)
    scale = lax.rsqrt(mean_square + EPSILON)
    scaled = message * jnp.concatenate([scale] * (hidden // width), axis=1) * gains
    stream = stream + dot(scaled.astype(BF16), update[0])
    final = stream.astype(BF16).reshape(nodes // 2, 2, members, hidden)
    rows = nodes // 2 * members
    change = dot_t(final[:, 0].reshape(rows, hidden), decode_even) + dot_t(
        final[:, 1].reshape(rows, hidden), decode_odd
    )
    wide = fields.astype(F32).reshape(nodes // 2, 2, half, width)
    even, odd = wide[:, 0], wide[:, 1]
    first = jnp.where(low, even, pltpu.roll(odd, channels, 2))
    second = jnp.where(low, pltpu.roll(even, channels, 2), odd)
    initial = jnp.concatenate([first, second], axis=1)
    forecast = (initial + change.reshape(initial.shape)).astype(BF16)
    for index, out in enumerate(outs):
        for pair in range(pairs):
            out[:, pair * width : (pair + 1) * width] = forecast[index * pairs + pair]


def weights_kernel(neighbours, own, before, after, down, up, from_after, from_before, *refs):
    *forecast, out, piece = refs
    forecast_kernel([0], *forecast, piece)
    rows, ensemble = own.shape
    first = from_before.shape[0] - rows
    row_count, column_count = lax.axis_size("member"), lax.axis_size("space")
    own_row, own_column = lax.axis_index("member"), lax.axis_index("space")
    targets, origins = partners("member")
    offsets = []
    for index in range(neighbours.shape[1]):
        region = neighbours[0, index]
        near_row = (region // column_count - own_row + 1 + row_count) % row_count - 1
        near_column = (region % column_count - own_column + 2 + column_count) % column_count - 2
        offsets.append((near_row, near_column))
    sources = {(0, -1): (before, 0), (0, 1): (after, 0), (0, -2): (from_before, first), (0, 2): (from_after, first)}
    for row, source in ((-1, up), (1, down)):
        for index in range(3):
            sources[row, index - 1] = (source, index * rows)
    total = own[...].astype(F32)
    for place, (source, start) in sources.items():
        weight = 0.0
        for near_row, near_column in offsets:
            here = jnp.logical_and(near_row == place[0], near_column == place[1])
            weight = weight + jnp.where(here, 1.0 / (1.0 + (place[0] ** 2 + place[1] ** 2) / 2.0), 0.0)
        total = total + weight * source[start : start + rows, :].astype(F32)
    identity = (
        lax.broadcasted_iota(jnp.int32, (ensemble, ensemble), 0)
        == lax.broadcasted_iota(jnp.int32, (ensemble, ensemble), 1)
    ).astype(F32)
    full = functools.partial(jnp.dot, precision=FULL_PRECISION, preferred_element_type=F32)
    system = identity + total[:ensemble] / (ensemble - 1)
    squares = jnp.sum(jnp.sum(system * system, axis=1, keepdims=True), axis=0, keepdims=True)
    scaling = jnp.sqrt(squares)
    iterate = system / scaling
    correction = 1.5 * identity - 0.5 * iterate
    inverse = correction
    for _ in range(ITERS_NS - 1):
        iterate = full(iterate, correction)
        correction = 1.5 * identity - 0.5 * full(inverse, iterate)
        inverse = full(correction, inverse)
    tail = total[ensemble:]
    forcing = jnp.broadcast_to(tail[0:1] + tail[1:2], (8, ensemble))
    mean_weights = full(full(forcing, inverse), inverse)[0:1] / (scaling * (ensemble - 1))
    transform = inverse / jnp.sqrt(scaling) + mean_weights
    rest = (1.0 - jnp.sum(transform, axis=1, keepdims=True)) / ensemble
    members = ensemble // row_count
    to_rows = lax.broadcasted_iota(jnp.int32, (ensemble, ensemble), 0)
    to_columns = lax.broadcasted_iota(jnp.int32, (ensemble, ensemble), 1)
    wanted_rows, wanted_columns = to_rows % members, to_columns % members
    for index in range(row_count):
        target, origin = targets[index] * members, origins[index] * members
        wanted_rows = wanted_rows + jnp.where(to_rows // members == index, target, 0)
        wanted_columns = wanted_columns + jnp.where(to_columns // members == index, origin, 0)
    by_row = (to_columns == wanted_rows).astype(F32).astype(BF16)
    by_column = (to_rows == wanted_columns).astype(F32).astype(BF16)
    for index, part in enumerate(split(transform + rest)):
        moved = dot(dot(by_row, part).astype(BF16), by_column)
        out[:, index * ensemble : (index + 1) * ensemble] = moved.astype(BF16)


def analysis_kernel(weights, *refs):
    count = len(refs) // 2
    pieces, outs = refs[:count][::-1], refs[count:]
    members, width = pieces[0].shape
    step_width = 512
    for start in range(0, width, step_width):
        columns = [piece[:, start : start + step_width] for piece in pieces]
        analysed = dot(weights[...], jnp.concatenate(columns * 2, axis=0)).astype(BF16)
        for index, out in enumerate(outs):
            out[:, start : start + step_width] = analysed[index * members : (index + 1) * members]


def stage(piece, region, staged):
    members, width = piece.shape
    half = members // 2
    lanes = staged.shape[2]
    low = lax.broadcasted_iota(jnp.int32, (half, lanes), 1) < lanes // 2
    for pair in range(width // lanes):
        block = piece[:, pair * lanes : (pair + 1) * lanes].astype(F32)
        first, second = block[:half], block[half:]
        row = 2 * pair * half
        staged[region, row : row + half, :] = jnp.where(low, first, pltpu.roll(second, lanes // 2, 1))
        staged[region, row + half : row + 2 * half, :] = jnp.where(low, pltpu.roll(first, lanes // 2, 1), second)


def stage_kernel(order, *refs):
    *pieces, staged = refs
    _, origins = partners("member")
    for index, piece in zip(order, pieces):
        stage(piece, origins[index], staged)


def output_kernel(last, piece, _, far, staged, out, sems):
    _, origins = partners("member")
    stage(piece, origins[last], staged)
    members, channels, nodes = out.shape
    half = members // 2
    chunk = nodes // len(origins)
    copies = []
    for pair in range(half):
        block = jnp.concatenate(
            [staged[region, pl.ds(pair, chunk, stride=half), :] for region in range(len(origins))], axis=0
        ).T.astype(BF16)
        out[pair] = block[:channels]
        out[pair + half] = block[channels:]
        if (pair + 1) % OUTPUT_STEP == 0:
            start = pair + 1 - OUTPUT_STEP
            parts = [slice(first, first + OUTPUT_STEP) for first in (start, start + half)]
            copies += start_copies(sems.at[pair // OUTPUT_STEP], *((out.at[part], far.at[part]) for part in parts))
    for copy in copies:
        copy.wait()


def ring(value, axis, shift):
    count = lax.axis_size(axis)
    return lax.ppermute(value, axis, [(i, (i + shift) % count) for i in range(count)])


def partners(axis):
    count = lax.axis_size(axis)
    own = lax.axis_index(axis)
    if count & (count - 1) == 0:
        targets = origins = [own ^ step for step in range(count)]
    else:
        targets = [lax.rem(own + step, count) for step in range(count)]
        origins = [lax.rem(own + count - step, count) for step in range(count)]
    return targets, origins


def exchange(pieces, axis):
    count = lax.axis_size(axis)
    paired_up = count & (count - 1) == 0
    return [pieces[0]] + [
        lax.ppermute(piece, axis, [(i, i ^ step if paired_up else (i + step) % count) for i in range(count)])
        for step, piece in enumerate(pieces)
        if step
    ]


def body(
    initial_fields,
    encode_weight,
    send_weight,
    receive_weight,
    update_weight,
    norm_gain,
    decode_weight,
    edge_senders,
    halo_nodes,
    observed_perturbation,
    observed_values,
    region_neighbours,
):
    members, channels, nodes = initial_fields.shape
    hidden = encode_weight.shape[1]
    half = members // 2
    halo_count = halo_nodes.shape[1]
    ensemble = observed_perturbation.shape[1]
    groups = lax.axis_size("member")
    rows = ensemble + TAIL
    struct = jax.ShapeDtypeStruct
    raw = (initial_fields, encode_weight, send_weight, receive_weight)
    own, *near = call(
        gram_kernel,
        (struct((rows, ensemble), BF16),) + tuple(pltpu.VMEM(value.shape, BF16) for value in raw),
        placed_in(pltpu.HBM, observed_perturbation, observed_values, halo_nodes, *raw),
        specs=[HBM] * 7,
        scratch=[
            pltpu.VMEM(observed_perturbation.shape, BF16),
            pltpu.VMEM(observed_values.shape, BF16),
            pltpu.VMEM(halo_nodes.shape, jnp.int32),
            pltpu.SemaphoreType.DMA((7,)),
        ],
        flops=1 << 24,
    )
    before = ring(own, "space", 1)
    fields, *weights = placed_in(pltpu.VMEM, *near)
    columns, rearranged = call(
        columns_kernel,
        (struct((half, nodes, 2 * channels), BF16), struct((nodes * half, 2 * channels), BF16)),
        (fields,),
        scratch=[pltpu.VMEM((nodes * half, 2 * channels), F32)],
        flops=1 << 28,
    )
    own_again, _ = lax.optimization_barrier((own, columns))
    after = ring(own_again, "space", -1)
    sent, received = call(
        own_kernel,
        (pltpu.VMEM((nodes + 1, members, hidden), F32), pltpu.VMEM((nodes, members, hidden), F32)),
        (rearranged, *weights),
        flops=1 << 30,
    )
    size = halo_count * half
    columns, sent, received = lax.optimization_barrier((columns, sent, received))
    to_before, to_after, column = call(
        functools.partial(pick_kernel, halo_count),
        (struct((size + rows, 2 * channels), BF16),) * 2 + (struct((3 * rows, ensemble), BF16),),
        (columns, own, before, after),
        scratch=[pltpu.VMEM((2 * size, 2 * channels), F32)],
        flops=1 << 27,
    )
    from_after = ring(to_before, "space", -1)
    from_before = ring(to_after, "space", 1)
    edges = edge_senders.T
    started, halo_edges = call(
        functools.partial(own_message_kernel, 2 * halo_count),
        (
            pltpu.VMEM((nodes + 1, members, hidden), F32),
            struct((edges.size + BATCH + 1,), jnp.int32),
        ),
        (edges, *placed_in(pltpu.VMEM, sent, received)),
        specs=[SMEM, VMEM, VMEM],
        outs=(VMEM, SMEM),
        flops=1 << 31,
    )
    column, started = lax.optimization_barrier((column, started))
    down = ring(column, "member", -1)
    up = ring(column, "member", 1)
    width = nodes // groups * channels
    piece = struct((members, width), BF16)
    shared = (rearranged, encode_weight, update_weight, norm_gain, decode_weight.T)
    *predicted, messages = call(
        functools.partial(message_kernel, halo_count),
        (piece,) * (groups - 1) + (pltpu.VMEM(started.shape, F32),),
        (
            halo_edges,
            rearranged,
            *placed_in(pltpu.VMEM, received, started),
            from_after,
            from_before,
            encode_weight,
            send_weight,
            update_weight,
            norm_gain,
            decode_weight.T,
        ),
        specs=[ANY] + [VMEM] * 10,
        scratch=[
            pltpu.VMEM((2 * halo_count, members, hidden), F32),
            pltpu.SMEM(halo_edges.shape, jnp.int32),
            pltpu.SemaphoreType.DMA((1,)),
        ],
        flops=1 << 32,
        aliases={3: groups - 1},
    )
    predicted = exchange([None, *predicted], "member")
    weights, kept = call(
        weights_kernel,
        (struct((ensemble, 2 * ensemble), BF16), piece),
        (
            region_neighbours,
            own,
            before,
            after,
            down,
            up,
            from_after,
            from_before,
            *placed_in(pltpu.VMEM, messages),
            *shared,
        ),
        specs=[SMEM] + [VMEM] * (8 + len(shared)),
        flops=1 << 30,
    )
    states = (kept, *predicted[1:])
    analysed = call(
        analysis_kernel,
        (piece,) * groups,
        (weights, *states[::-1]),
        flops=1 << 28,
    )
    returned = exchange(analysed, "member")
    *order, last = [*range(1, groups)][::-1]
    order = [*order, 0]
    staged = call(
        functools.partial(stage_kernel, order),
        pltpu.VMEM((groups, nodes // groups * half, 2 * channels), F32),
        tuple(returned[index] for index in order),
        flops=1 << 24,
    )
    analysis, _ = call(
        functools.partial(output_kernel, last),
        (struct((members, channels, nodes), BF16), pltpu.VMEM(staged.shape, F32)),
        (returned[last], *placed_in(pltpu.VMEM, staged)),
        outs=(HBM, VMEM),
        scratch=[
            pltpu.VMEM((members, channels, nodes), BF16),
            pltpu.SemaphoreType.DMA((half // OUTPUT_STEP, 2)),
        ],
        flops=1 << 24,
        aliases={1: 1},
    )
    return analysis


def solution(mesh):
    placed = (
        P("member", None, "space"),
        P(),
        P(),
        P(),
        P(),
        P(),
        P(),
        P("space", None),
        P(None, "space"),
        P(("member", "space"), None, None),
        P(("member", "space"), None, None),
        P(("member", "space"), None),
    )
    return jax.shard_map(
        body, mesh=mesh, in_specs=placed, out_specs=P("member", None, "space"), check_vma=False
    )
```
